256 devices in a mesh: tp: 4 (over y_hi, core), client: 4 (over x), region: 16 (over z, y_lo).
Axes of the slice: x: 4, y: 4 (y_hi: 2, y_lo: 2; y = y_hi * 2 + y_lo), z: 8, core: 2. Of those that a mesh axis runs over, the one named last changes fastest.
Arguments:
- hidden_in: bfloat16 [64, 2, 128, 1792], P(('client', 'region'), None, None, 'tp'), may hold values from -6 to 6
- target: bfloat16 [64, 2, 128, 1792], P(('client', 'region'), None, None, 'tp'), may hold values from -38 to 38, as said below
- up_weight: bfloat16 [1792, 7168], P(None, 'tp'), may hold values from -1 to 1
- down_weight: bfloat16 [7168, 1792], P('tp'), may hold values from -0.0625 to 0.0625
- noise_up: float32 [1792, 7168], P(('client', 'region'), 'tp'), may hold values from -6 to 6
- noise_down: float32 [7168, 1792], P('tp', ('client', 'region')), may hold values from -6 to 6
Outputs:
- new_up: float32 [1792, 7168], P(('client', 'region'), 'tp')
- new_down: float32 [7168, 1792], P('tp', ('client', 'region'))
The draws below stay inside these ranges and needn't reach their ends.
Inputs may be any that keep to these rules, and one draw needn't show every extreme that they name: `target`: targets of every client and step.
All inputs are finite; a program needn't handle non-finite values.
Results may differ from the reference program's by a relative error of at most 0.014.
Values may be sent and summed in bfloat16 or wider, within the bound.
No kernel may reach another device: no remote copies, remote signals or barrier semaphores. Data moves between devices by JAX's collectives and lax.ppermute only.
A program may use at most 128 MiB of HBM per device.

```python
import math
import jax
import jax.numpy as jnp
from jax import lax

D = 1792
F = 7168
TOK = 128
STEPS = 2
CLIENTS = 64
N_CLIENT = 4
N_REGION = 16


def shared_states(key):
    first = jax.random.fold_in(key, 0)
    shape = (CLIENTS, STEPS, TOK, D)
    normal_part = jax.random.truncated_normal(first, -6.0, 6.0, shape, jnp.float32)
    return normal_part


def draw_hidden_in(key, part):
    states = shared_states(key)
    return states.astype(jnp.bfloat16)


def draw_target(key, part):
    states = shared_states(key)
    key = jax.random.fold_in(key, 11)
    key_order, key_jitter, key_noise = jax.random.split(key, 3)
    order = jax.random.permutation(key_order, CLIENTS).astype(jnp.float32)
    jitter = jax.random.uniform(key_jitter, (CLIENTS,), jnp.float32)
    spread = (order + jitter) / CLIENTS
    lowest = 0.03
    ratio = math.log(8.0 / lowest)
    client_scale = lowest * jnp.exp(spread * ratio)
    noise = jax.random.truncated_normal(key_noise, -4.0, 4.0, (CLIENTS, STEPS, TOK, D), jnp.float32)
    goals = states + client_scale[:, None, None, None] * noise
    return goals.astype(jnp.bfloat16)


def draw_up_weight(key, part):
    key = jax.random.fold_in(key, 23)
    deviation = 0.2 / math.sqrt(D)
    values = deviation * jax.random.truncated_normal(key, -4.0, 4.0, (D, F), jnp.float32)
    return values.astype(jnp.bfloat16)


def levels(own_key, extent, cuts, smallest, largest):
    def one(axis_at, parts):
        heights = jax.random.uniform(jax.random.fold_in(jax.random.fold_in(own_key, 6), axis_at), (parts,), jnp.float32, smallest / len(cuts), largest / len(cuts))
        return jnp.repeat(jnp.exp(heights), extent[axis_at] // parts).reshape((-1,) + (1,) * (len(extent) - axis_at - 1))

    loudness = one(*cuts[0])
    for cut in cuts[1:]:
        loudness = loudness * one(*cut)
    return loudness


def scatter_about(own_key, extent, scale, limit, cuts=(), held_as=jnp.bfloat16):
    drawn = jax.random.normal(own_key, extent, jnp.float32) * scale
    if len(cuts) > 0:
        drawn = levels(own_key, extent, cuts, -0.22, 0.18) * drawn
    return jnp.clip(drawn, min=-limit, max=limit).astype(held_as)


def setup_inputs(seed: int = 0) -> dict:
    key_of = jax.random.split(jax.random.key(seed), 7)
    hidden_in = draw_hidden_in(jax.random.fold_in(key_of[6], 71), 0)
    target = draw_target(jax.random.fold_in(key_of[6], 71), 0)
    up_weight = draw_up_weight(jax.random.fold_in(key_of[6], 71), 0)
    down_weight = scatter_about(key_of[3], (F, D), F ** -0.5, 0.0625, ((0, 4),))
    noise_up = scatter_about(key_of[4], (D, F), 1.0, 6.0, ((0, 64), (1, 4)), jnp.float32)
    noise_down = scatter_about(key_of[5], (F, D), 1.0, 6.0, ((0, 4), (1, 64)), jnp.float32)
    return {"hidden_in": hidden_in, "target": target, "up_weight": up_weight, "down_weight": down_weight, "noise_up": noise_up, "noise_down": noise_down}


local_rate = 0.5
clip_rms = 0.08
server_rate = 0.02

def gelu_back(pre, back):
    return jax.vjp(lambda value: jax.nn.gelu(value, approximate=True), pre)[1](back)[0]

def gradients(inputs, goals, w_up, w_down):
    xfloat = inputs.astype(jnp.float32)
    normed = (xfloat * lax.rsqrt(lax.optimization_barrier(jnp.mean(xfloat * xfloat, axis=-1, keepdims=True)) + 1e-06)).astype(jnp.bfloat16)
    pre = jnp.dot(normed, w_up, preferred_element_type=jnp.float32)
    act = jax.nn.gelu(pre, approximate=True).astype(jnp.bfloat16)
    output = xfloat + jnp.dot(act, w_down, preferred_element_type=jnp.float32)
    resid = ((output - goals.astype(jnp.float32)) / inputs.shape[0]).astype(jnp.bfloat16)
    grad_down = jnp.dot(act.T, resid, preferred_element_type=jnp.float32)
    back = jnp.dot(resid, w_down.T, preferred_element_type=jnp.float32)
    dpre = gelu_back(pre, back).astype(jnp.bfloat16)
    grad_up = jnp.dot(normed.T, dpre, preferred_element_type=jnp.float32)
    return (grad_up, grad_down)

def reference(hidden_in, target, up_weight, down_weight, noise_up, noise_down):
    bound = clip_rms * math.sqrt(2.0 * D * F)

    def per_client(carry, pair):
        inputs, goals = pair
        w_up, w_down = (up_weight, down_weight)
        acc_up = jnp.zeros((D, F), jnp.float32)
        acc_down = jnp.zeros((F, D), jnp.float32)
        for turn in range(STEPS):
            grad_up, grad_down = gradients(inputs[turn], goals[turn], w_up, w_down)
            acc_up = acc_up + grad_up
            acc_down = acc_down + grad_down
            w_up = (w_up.astype(jnp.float32) - local_rate * grad_up).astype(jnp.bfloat16)
            w_down = (w_down.astype(jnp.float32) - local_rate * grad_down).astype(jnp.bfloat16)
        delta_up = -local_rate * acc_up
        delta_down = -local_rate * acc_down
        size = jnp.sqrt(jnp.sum(delta_up * delta_up) + jnp.sum(delta_down * delta_down))
        factor = bound / jnp.maximum(size, bound)
        clip_up = lax.optimization_barrier((delta_up * factor).astype(jnp.bfloat16)).astype(jnp.float32)
        clip_down = lax.optimization_barrier((delta_down * factor).astype(jnp.bfloat16)).astype(jnp.float32)
        return ((carry[0] + clip_up, carry[1] + clip_down), None)
    start = (jnp.zeros((D, F), jnp.float32), jnp.zeros((F, D), jnp.float32))
    totals, unused = lax.scan(per_client, start, (hidden_in, target))
    root = math.sqrt(N_CLIENT * N_REGION)
    scale = server_rate / (clip_rms * root)
    new_up = up_weight.astype(jnp.float32) + scale * (totals[0] + clip_rms * root * noise_up)
    new_down = down_weight.astype(jnp.float32) + scale * (totals[1] + clip_rms * root * noise_down)
    return (new_up, new_down)
```

```python
import math

import jax
import jax.numpy as jnp
from jax import lax
from jax.sharding import PartitionSpec as P

D = 1792
F = 7168
TOK = 128
HALF = 896
BLOCK = 56

local_rate = 0.5
clip_rms = 0.08
server_rate = 0.02

X_UP = [(i, (i + 1) % 4) for i in range(4)]
X_DOWN = [(i, (i + 3) % 4) for i in range(4)]
Z_UP = [(i, (i + 2) % 16) for i in range(16)]
Z_DOWN = [(i, (i + 14) % 16) for i in range(16)]
Y_SWAP = [(i, i ^ 1) for i in range(16)]
CORE_SWAP = [(i, i ^ 1) for i in range(4)]
FAR_SWAP = [(i, i ^ 2) for i in range(4)]

f32 = jnp.float32
bf16 = jnp.bfloat16


def gelu_back(pre, back):
    return jax.vjp(lambda value: jax.nn.gelu(value, approximate=True), pre)[1](back)[0]


def mm(left, right):
    return jnp.dot(left, right, preferred_element_type=f32)


def mm_nt(left, right):
    return lax.dot_general(left, right, (((1,), (1,)), ((), ())), preferred_element_type=f32)


def mm_split(left, right):
    high = left.astype(bf16)
    low = (left - high.astype(f32)).astype(bf16)
    return mm(high, right) + mm(low, right)


def sum_over_tp(part, core):
    halves = part.reshape(2, TOK // 2, D)
    mine = jnp.where(core == 0, halves[0], halves[1])
    other = jnp.where(core == 0, halves[1], halves[0]).astype(bf16)
    got = lax.ppermute(other, "tp", CORE_SWAP).astype(f32)
    chip = (mine + got).astype(bf16)
    far = lax.ppermute(chip, "tp", FAR_SWAP)
    total = ((chip.astype(f32) + far.astype(f32)) * (1.0 / TOK)).astype(bf16)
    back = lax.ppermute(total, "tp", CORE_SWAP)
    first = jnp.where(core == 0, total, back)
    second = jnp.where(core == 0, back, total)
    return jnp.concatenate([first, second], axis=0)


def ring(piece, axis, up, down, me, n):
    far = n // 2
    opposite = piece((me + far) % n)
    from_down = lax.ppermute(opposite[..., :HALF].astype(bf16), axis, up)
    from_up = lax.ppermute(opposite[..., HALF:].astype(bf16), axis, down)
    for distance in range(far - 1, 0, -1):
        ahead = piece((me + distance) % n)
        behind = piece((me + n - distance) % n)
        if distance == far - 1:
            ahead = jnp.concatenate(
                [ahead[..., :HALF] + from_down.astype(f32), ahead[..., HALF:]], axis=-1
            )
            behind = jnp.concatenate(
                [behind[..., :HALF], behind[..., HALF:] + from_up.astype(f32)], axis=-1
            )
        else:
            ahead = ahead + from_down.astype(f32)
            behind = behind + from_up.astype(f32)
        from_down = lax.ppermute(ahead.astype(bf16), axis, up)
        from_up = lax.ppermute(behind.astype(bf16), axis, down)
    return piece(me) + from_down.astype(f32) + from_up.astype(f32)


def swap_y(block, y_lo):
    halves = block.reshape(2, BLOCK // 2, D)
    mine = jnp.where(y_lo == 0, halves[0], halves[1])
    other = jnp.where(y_lo == 0, halves[1], halves[0]).astype(bf16)
    return mine + lax.ppermute(other, "region", Y_SWAP).astype(f32)


def shards(hidden_in, target, up_weight, down_weight, noise_up, noise_down):
    tp = lax.axis_index("tp")
    core = tp % 2
    client = lax.axis_index("client")
    region = lax.axis_index("region")
    z = region // 2
    y_lo = region % 2

    own = jnp.swapaxes(hidden_in[0], 1, 2)
    goal = jnp.swapaxes(target[0], 1, 2)
    states = lax.all_gather(own, "tp", axis=1, tiled=True)
    xfloat = states.astype(f32)
    normed_t = (
        xfloat * lax.rsqrt(jnp.mean(xfloat * xfloat, axis=1, keepdims=True) + 1e-06)
    ).astype(bf16)
    normed_t = jnp.concatenate([normed_t[0], normed_t[1]], axis=1)
    normed = normed_t.T

    gap = own.astype(f32) - goal.astype(f32)
    gaps = lax.dynamic_update_slice(
        jnp.zeros((2, D, TOK), f32), gap, (0, tp * (D // 4), 0)
    )
    gaps = jnp.swapaxes(gaps, 1, 2)

    pre = mm(normed, up_weight)
    pre_1 = pre[:TOK]
    act_1 = jax.nn.gelu(pre_1, approximate=True).astype(bf16)
    resid_1 = sum_over_tp(mm(act_1, down_weight) + gaps[0], core)
    back_1 = mm_nt(resid_1, down_weight)
    dpre_1 = gelu_back(pre_1, back_1).astype(bf16)

    gram_normed = mm_nt(normed, normed)
    pre_2 = pre[TOK:] - local_rate * mm_split(gram_normed[TOK:, :TOK], dpre_1)
    act_2 = jax.nn.gelu(pre_2, approximate=True).astype(bf16)
    acts = jnp.concatenate([act_1, act_2], axis=0)
    gram_act = mm_nt(acts, acts)
    part_2 = (
        mm(act_2, down_weight)
        - local_rate * mm_split(gram_act[TOK:, :TOK], resid_1)
        + gaps[1]
    )
    resid_2 = sum_over_tp(part_2, core)
    resids = jnp.concatenate([resid_1, resid_2], axis=0)
    gram_resid = mm_nt(resids, resids)
    back_2 = mm_nt(resid_2, down_weight) - local_rate * mm_split(
        gram_resid[TOK:, :TOK], act_1
    )
    dpre_2 = gelu_back(pre_2, back_2).astype(bf16)
    dpres = jnp.concatenate([dpre_1, dpre_2], axis=0)
    gram_dpre = mm_nt(dpres, dpres)

    squared = (local_rate * local_rate) * (
        jnp.sum(gram_normed * gram_dpre) + jnp.sum(gram_resid * gram_act)
    )
    squared = jnp.full((8, 128), squared, f32)
    squared = squared + lax.ppermute(squared, "tp", CORE_SWAP)
    squared = squared + lax.ppermute(squared, "tp", FAR_SWAP)
    squared = squared[0, 0]
    bound = clip_rms * math.sqrt(2.0 * D * F)
    factor = bound / jnp.maximum(jnp.sqrt(squared), bound)
    scale_own = -local_rate * factor

    rows_up = normed_t.reshape(4, 8, BLOCK, 2 * TOK)
    rows_down = resids.T.reshape(4, 8, BLOCK, 2 * TOK)

    def up_piece(k):
        rows = lax.dynamic_index_in_dim(rows_up, k, 0, keepdims=False)
        return scale_own * mm(rows.reshape(8 * BLOCK, 2 * TOK), dpres)

    def down_piece(k):
        rows = lax.dynamic_index_in_dim(rows_down, k, 1, keepdims=False)
        return scale_own * mm(rows.reshape(4 * BLOCK, 2 * TOK), acts)

    up_x = ring(up_piece, "client", X_UP, X_DOWN, client, 4)
    down_z = ring(down_piece, "region", Z_UP, Z_DOWN, z, 8)
    up_x = up_x.reshape(8, BLOCK, D)
    down_z = down_z.reshape(4, BLOCK, D)

    def at(array):
        return lambda k: lax.dynamic_index_in_dim(array, k, 0, keepdims=False)

    up_z = ring(at(up_x), "region", Z_UP, Z_DOWN, z, 8)
    down_x = ring(at(down_z), "client", X_UP, X_DOWN, client, 4)
    total_up = swap_y(up_z, y_lo)
    total_down = swap_y(down_x, y_lo).T

    count = 64
    rows = D // count
    block = client * 16 + region
    base_up = lax.dynamic_slice_in_dim(up_weight, block * rows, rows, 0).astype(f32)
    base_down = lax.dynamic_slice_in_dim(down_weight, block * rows, rows, 1).astype(f32)
    root = math.sqrt(count)
    scale = server_rate / (clip_rms * root)
    new_up = base_up + scale * (total_up + clip_rms * root * noise_up)
    new_down = base_down + scale * (total_down + clip_rms * root * noise_down)
    return (new_up, new_down)


def solution(mesh):
    placed = (
        P(("client", "region"), None, None, "tp"),
        P(("client", "region"), None, None, "tp"),
        P(None, "tp"),
        P("tp", None),
        P(("client", "region"), "tp"),
        P("tp", ("client", "region")),
    )
    return jax.shard_map(
        shards,
        mesh=mesh,
        in_specs=placed,
        out_specs=(P(("client", "region"), "tp"), P("tp", ("client", "region"))),
        check_vma=False,
    )
```

```python
import math

import jax
import jax.numpy as jnp
from jax import lax
from jax.experimental import pallas as pl
from jax.experimental.pallas import tpu as pltpu
from jax.sharding import PartitionSpec as P

D = 1792
F = 7168
TOK = 128
HALF = 896
BLOCK = 56
PART = 256
ROOT_2_PI = math.sqrt(2.0 / math.pi)

local_rate = 0.5
clip_rms = 0.08
server_rate = 0.02

X_UP = [(i, (i + 1) % 4) for i in range(4)]
X_DOWN = [(i, (i + 3) % 4) for i in range(4)]
Z_UP = [(i, (i + 2) % 16) for i in range(16)]
Z_DOWN = [(i, (i + 14) % 16) for i in range(16)]
Y_SWAP = [(i, i ^ 1) for i in range(16)]
CORE_SWAP = [(i, i ^ 1) for i in range(4)]
FAR_SWAP = [(i, i ^ 2) for i in range(4)]

f32 = jnp.float32
bf16 = jnp.bfloat16


def mm(left, right):
    return jnp.dot(left, right, preferred_element_type=f32)


def mm_nt(left, right):
    return lax.dot_general(left, right, (((1,), (1,)), ((), ())), preferred_element_type=f32)


def mm_split(left, right):
    high = left.astype(bf16)
    low = (left - high.astype(f32)).astype(bf16)
    return mm(high, right) + mm(low, right)


def gelu_parts(pre):
    square = pre * pre
    curve = jnp.tanh(ROOT_2_PI * (pre + 0.044715 * pre * square))
    value = 0.5 * pre * (1.0 + curve)
    slope = 0.5 * (1.0 + curve) + 0.5 * pre * (1.0 - curve * curve) * (
        ROOT_2_PI * (1.0 + 3.0 * 0.044715 * square)
    )
    return value, slope


def place_gap(core_ref, own_ref, goal_ref, step, wide):
    wide[...] = jnp.zeros_like(wide)
    start = pl.multiple_of(core_ref[0] * (D // 4), 64)
    wide[pl.ds(start, D // 4), :] = own_ref[step].astype(f32) - goal_ref[step].astype(f32)
    return wide[...].T


def hand_out(core_ref, total, keep_ref, send_ref):
    core = core_ref[0] % 2
    half = TOK // 2
    keep_ref[...] = total[pl.ds(pl.multiple_of(core * half, half), half), :]
    other = total[pl.ds(pl.multiple_of((1 - core) * half, half), half), :]
    send_ref[...] = other.astype(bf16)


def take_in(core_ref, mine_ref, other_ref, resid):
    core = core_ref[0] % 2
    half = TOK // 2
    resid[pl.ds(pl.multiple_of(core * half, half), half), :] = mine_ref[...]
    resid[pl.ds(pl.multiple_of((1 - core) * half, half), half), :] = other_ref[...]


def first_kernel(
    core_ref, x_ref, own_ref, goal_ref, up_ref, down_ref,
    normed_t_ref, pre_ref, act_ref, gram_ref, keep_ref, send_ref,
    normed, total, wide,
):
    j = pl.program_id(0)

    @pl.when(j == 0)
    def _():
        xfloat = x_ref[...].astype(f32)
        mean = jnp.mean(xfloat * xfloat, axis=0, keepdims=True)
        scaled = (xfloat * lax.rsqrt(mean + 1e-06)).astype(bf16)
        normed_t_ref[...] = scaled
        flat = scaled.T
        normed[...] = flat
        gram_ref[...] = mm_nt(flat, flat)
        total[...] = place_gap(core_ref, own_ref, goal_ref, 0, wide)

    pre = mm(normed[...], up_ref[...])
    pre_ref[...] = pre
    act = gelu_parts(pre[:TOK])[0].astype(bf16)
    act_ref[...] = act
    total[...] += mm(act, down_ref[...])

    @pl.when(j == pl.num_programs(0) - 1)
    def _():
        hand_out(core_ref, total, keep_ref, send_ref)


def second_kernel(
    core_ref, mine_ref, other_ref, own_ref, goal_ref, down_ref, pre_ref, act_ref, gram_ref,
    resid_ref, resid_t_ref, dpre_ref, pre_2_ref, act_2_ref, keep_ref, send_ref,
    total, wide, cross,
):
    j = pl.program_id(0)

    @pl.when(j == 0)
    def _():
        take_in(core_ref, mine_ref, other_ref, resid_ref)
        total[...] = place_gap(core_ref, own_ref, goal_ref, 1, wide)
        cross[...] = jnp.zeros_like(cross)
        resid_t_ref[...] = resid_ref[...].T

    back = mm_nt(resid_ref[...], down_ref[...])
    dpre = (back * gelu_parts(pre_ref[:TOK, :])[1]).astype(bf16)
    dpre_ref[...] = dpre
    pre_2 = pre_ref[TOK:, :] - local_rate * mm_split(gram_ref[TOK:, :TOK], dpre)
    pre_2_ref[...] = pre_2
    act_2 = gelu_parts(pre_2)[0].astype(bf16)
    act_2_ref[...] = act_2
    total[...] += mm(act_2, down_ref[...])
    cross[...] += mm_nt(act_2, act_ref[...])

    @pl.when(j == pl.num_programs(0) - 1)
    def _():
        total[...] -= local_rate * mm_split(cross[...], resid_ref[...])
        hand_out(core_ref, total, keep_ref, send_ref)


def third_kernel(
    core_ref, mine_ref, other_ref, resid_ref, down_ref, act_ref, act_2_ref, pre_2_ref, dpre_ref, gram_ref,
    resid_t_ref, dpre_2_ref, squared_ref,
    resid_2, gram_resid, gram_act, gram_dpre,
):
    j = pl.program_id(0)

    @pl.when(j == 0)
    def _():
        take_in(core_ref, mine_ref, other_ref, resid_2)
        both = jnp.concatenate([resid_ref[...], resid_2[...]], axis=0)
        gram_resid[...] = mm_nt(both, both)
        gram_act[...] = jnp.zeros_like(gram_act)
        gram_dpre[...] = jnp.zeros_like(gram_dpre)
        resid_t_ref[...] = resid_2[...].T

    back = mm_nt(resid_2[...], down_ref[...]) - local_rate * mm_split(
        gram_resid[TOK:, :TOK], act_ref[...]
    )
    dpre_2 = (back * gelu_parts(pre_2_ref[...])[1]).astype(bf16)
    dpre_2_ref[...] = dpre_2
    acts = jnp.concatenate([act_ref[...], act_2_ref[...]], axis=0)
    gram_act[...] += mm_nt(acts, acts)
    dpres = jnp.concatenate([dpre_ref[...], dpre_2], axis=0)
    gram_dpre[...] += mm_nt(dpres, dpres)

    @pl.when(j == pl.num_programs(0) - 1)
    def _():
        terms = gram_ref[...] * gram_dpre[...] + gram_resid[...] * gram_act[...]
        squared_ref[...] = jnp.full((8, 128), (local_rate * local_rate) * jnp.sum(terms), f32)


def whole(shape):
    return pl.BlockSpec(shape, lambda j: (0,) * len(shape))


def columns(rows):
    return pl.BlockSpec((rows, PART), lambda j: (0, j))


DOWN_ROWS = pl.BlockSpec((PART, D), lambda j: (j, 0))
SCALAR = pl.BlockSpec(memory_space=pltpu.SMEM)
HALF_TOK = (TOK // 2, D)


def call(kernel, in_specs, out_specs, out_types, scratch, flops, moved):
    return pl.pallas_call(
        kernel,
        grid=(D // PART,),
        in_specs=in_specs,
        out_specs=out_specs,
        out_shape=[jax.ShapeDtypeStruct(*kind) for kind in out_types],
        scratch_shapes=[pltpu.VMEM(*kind) for kind in scratch],
        compiler_params=pltpu.CompilerParams(vmem_limit_bytes=40 * 1024 * 1024),
        cost_estimate=pl.CostEstimate(flops=flops, bytes_accessed=moved, transcendentals=0),
    )


def reduce_over_tp(keep, send):
    got = lax.ppermute(send, "tp", CORE_SWAP).astype(f32)
    chip = (keep + got).astype(bf16)
    far = lax.ppermute(chip, "tp", FAR_SWAP)
    mine = ((chip.astype(f32) + far.astype(f32)) * (1.0 / TOK)).astype(bf16)
    return mine, lax.ppermute(mine, "tp", CORE_SWAP)


def ring(piece, axis, up, down, me, n):
    far = n // 2
    opposite = piece((me + far) % n)
    from_down = lax.ppermute(opposite[..., :HALF].astype(bf16), axis, up)
    from_up = lax.ppermute(opposite[..., HALF:].astype(bf16), axis, down)
    for distance in range(far - 1, 0, -1):
        ahead = piece((me + distance) % n)
        behind = piece((me + n - distance) % n)
        if distance == far - 1:
            ahead = jnp.concatenate(
                [ahead[..., :HALF] + from_down.astype(f32), ahead[..., HALF:]], axis=-1
            )
            behind = jnp.concatenate(
                [behind[..., :HALF], behind[..., HALF:] + from_up.astype(f32)], axis=-1
            )
        else:
            ahead = ahead + from_down.astype(f32)
            behind = behind + from_up.astype(f32)
        from_down = lax.ppermute(ahead.astype(bf16), axis, up)
        from_up = lax.ppermute(behind.astype(bf16), axis, down)
    return piece(me) + from_down.astype(f32) + from_up.astype(f32)


def swap_y(block, y_lo):
    halves = block.reshape(2, BLOCK // 2, D)
    mine = jnp.where(y_lo == 0, halves[0], halves[1])
    other = jnp.where(y_lo == 0, halves[1], halves[0]).astype(bf16)
    return mine + lax.ppermute(other, "region", Y_SWAP).astype(f32)


def shards(hidden_in, target, up_weight, down_weight, noise_up, noise_down):
    tp = lax.axis_index("tp")
    client = lax.axis_index("client")
    region = lax.axis_index("region")
    z = region // 2
    y_lo = region % 2

    own = jnp.swapaxes(hidden_in[0], 1, 2)
    goal = jnp.swapaxes(target[0], 1, 2)
    states = lax.all_gather(
        jnp.concatenate([own[0], own[1]], axis=1), "tp", axis=0, tiled=True
    )
    spot = tp.astype(jnp.int32).reshape(1)
    narrow = whole((2, D // 4, TOK))

    normed_t, pre, act_1, gram, keep, send = call(
        first_kernel,
        [SCALAR, whole((D, 2 * TOK)), narrow, narrow, columns(D), DOWN_ROWS],
        [whole((D, 2 * TOK)), columns(2 * TOK), columns(TOK), whole((2 * TOK, 2 * TOK)), whole(HALF_TOK), whole(HALF_TOK)],
        [((D, 2 * TOK), bf16), ((2 * TOK, D), f32), ((TOK, D), bf16), ((2 * TOK, 2 * TOK), f32), (HALF_TOK, f32), (HALF_TOK, bf16)],
        [((2 * TOK, D), bf16), ((TOK, D), f32), ((D, TOK), f32)],
        6 * TOK * D * D, 4 * D * D,
    )(spot, states, own, goal, up_weight, down_weight)
    mine, other = reduce_over_tp(keep, send)

    resid_1, resid_t_1, dpre_1, pre_2, act_2, keep, send = call(
        second_kernel,
        [SCALAR, whole(HALF_TOK), whole(HALF_TOK), narrow, narrow, DOWN_ROWS, columns(2 * TOK), columns(TOK), whole((2 * TOK, 2 * TOK))],
        [whole((TOK, D)), whole((D, TOK)), columns(TOK), columns(TOK), columns(TOK), whole(HALF_TOK), whole(HALF_TOK)],
        [((TOK, D), bf16), ((D, TOK), bf16), ((TOK, D), bf16), ((TOK, D), f32), ((TOK, D), bf16), (HALF_TOK, f32), (HALF_TOK, bf16)],
        [((TOK, D), f32), ((D, TOK), f32), ((TOK, TOK), f32)],
        4 * TOK * D * D, 2 * D * D,
    )(spot, mine, other, own, goal, down_weight, pre, act_1, gram)
    mine, other = reduce_over_tp(keep, send)

    resid_t_2, dpre_2, squared = call(
        third_kernel,
        [SCALAR, whole(HALF_TOK), whole(HALF_TOK), whole((TOK, D)), DOWN_ROWS, columns(TOK), columns(TOK), columns(TOK), columns(TOK), whole((2 * TOK, 2 * TOK))],
        [whole((D, TOK)), columns(TOK), whole((8, 128))],
        [((D, TOK), bf16), ((TOK, D), bf16), ((8, 128), f32)],
        [((TOK, D), bf16)] + [((2 * TOK, 2 * TOK), f32)] * 3,
        2 * TOK * D * D, 2 * D * D,
    )(spot, mine, other, resid_1, down_weight, act_1, act_2, pre_2, dpre_1, gram)
    acts = jnp.concatenate([act_1, act_2], axis=0)
    dpres = jnp.concatenate([dpre_1, dpre_2], axis=0)
    resids_t = jnp.concatenate([resid_t_1, resid_t_2], axis=1)

    squared = squared + lax.ppermute(squared, "tp", CORE_SWAP)
    squared = squared + lax.ppermute(squared, "tp", FAR_SWAP)
    squared = squared[0, 0]
    bound = clip_rms * math.sqrt(2.0 * D * F)
    factor = bound / jnp.maximum(jnp.sqrt(squared), bound)
    scale_own = -local_rate * factor

    rows_up = normed_t.reshape(4, 8, BLOCK, 2 * TOK)
    rows_down = resids_t.reshape(4, 8, BLOCK, 2 * TOK)

    def up_piece(k):
        rows = lax.dynamic_index_in_dim(rows_up, k, 0, keepdims=False)
        return scale_own * mm(rows.reshape(8 * BLOCK, 2 * TOK), dpres)

    def down_piece(k):
        rows = lax.dynamic_index_in_dim(rows_down, k, 1, keepdims=False)
        return scale_own * mm(rows.reshape(4 * BLOCK, 2 * TOK), acts)

    up_x = ring(up_piece, "client", X_UP, X_DOWN, client, 4)
    down_z = ring(down_piece, "region", Z_UP, Z_DOWN, z, 8)
    up_x = up_x.reshape(8, BLOCK, D)
    down_z = down_z.reshape(4, BLOCK, D)

    def at(array):
        return lambda k: lax.dynamic_index_in_dim(array, k, 0, keepdims=False)

    up_z = ring(at(up_x), "region", Z_UP, Z_DOWN, z, 8)
    down_x = ring(at(down_z), "client", X_UP, X_DOWN, client, 4)
    total_up = swap_y(up_z, y_lo)
    total_down = swap_y(down_x, y_lo).T

    count = 64
    rows = D // count
    block = client * 16 + region
    base_up = lax.dynamic_slice_in_dim(up_weight, block * rows, rows, 0).astype(f32)
    base_down = lax.dynamic_slice_in_dim(down_weight, block * rows, rows, 1).astype(f32)
    root = math.sqrt(count)
    scale = server_rate / (clip_rms * root)
    new_up = base_up + scale * (total_up + clip_rms * root * noise_up)
    new_down = base_down + scale * (total_down + clip_rms * root * noise_down)
    return (new_up, new_down)


def solution(mesh):
    placed = (
        P(("client", "region"), None, None, "tp"),
        P(("client", "region"), None, None, "tp"),
        P(None, "tp"),
        P("tp", None),
        P(("client", "region"), "tp"),
        P("tp", ("client", "region")),
    )
    return jax.shard_map(
        shards,
        mesh=mesh,
        in_specs=placed,
        out_specs=(P(("client", "region"), "tp"), P("tp", ("client", "region"))),
        check_vma=False,
    )
```

```python
import math

import jax
import jax.numpy as jnp
from jax import lax
from jax.experimental import pallas as pl
from jax.experimental.pallas import tpu as pltpu
from jax.sharding import PartitionSpec as P

D = 1792
F = 7168
TOK = 128
HALF = 896
BLOCK = 56
PART = 256
ROOT_2_PI = math.sqrt(2.0 / math.pi)

local_rate = 0.5
clip_rms = 0.08
server_rate = 0.02

X_BY = [[(i, (i + d) % 4) for i in range(4)] for d in range(4)]
Z_UP = [(i, (i + 2) % 16) for i in range(16)]
Z_DOWN = [(i, (i + 14) % 16) for i in range(16)]
Y_SWAP = [(i, i ^ 1) for i in range(16)]
CORE_SWAP = [(i, i ^ 1) for i in range(4)]
FAR_SWAP = [(i, i ^ 2) for i in range(4)]

f32 = jnp.float32
bf16 = jnp.bfloat16
hold = lax.optimization_barrier


def mm(left, right):
    return jnp.dot(left, right, preferred_element_type=f32)


def mm_nt(left, right):
    return lax.dot_general(left, right, (((1,), (1,)), ((), ())), preferred_element_type=f32)


def mm_split(left, right):
    high = left.astype(bf16)
    low = (left - high.astype(f32)).astype(bf16)
    return mm(high, right) + mm(low, right)


def gelu_parts(pre):
    square = pre * pre
    curve = jnp.tanh(ROOT_2_PI * (pre + 0.044715 * pre * square))
    value = 0.5 * pre * (1.0 + curve)
    slope = 0.5 * (1.0 + curve) + 0.5 * pre * (1.0 - curve * curve) * (
        ROOT_2_PI * (1.0 + 3.0 * 0.044715 * square)
    )
    return value, slope


def place_gap(core_ref, own_ref, goal_ref, step, wide):
    wide[...] = jnp.zeros_like(wide)
    start = pl.multiple_of(core_ref[0] * (D // 4), 64)
    wide[pl.ds(start, D // 4), :] = own_ref[step].astype(f32) - goal_ref[step].astype(f32)
    return wide[...].T


def hand_out(core_ref, total, keep_ref, send_ref):
    core = core_ref[0] % 2
    half = TOK // 2
    keep_ref[...] = total[pl.ds(pl.multiple_of(core * half, half), half), :]
    other = total[pl.ds(pl.multiple_of((1 - core) * half, half), half), :]
    send_ref[...] = other.astype(bf16)


def take_in(core_ref, mine_ref, other_ref, resid):
    core = core_ref[0] % 2
    half = TOK // 2
    resid[pl.ds(pl.multiple_of(core * half, half), half), :] = mine_ref[...]
    resid[pl.ds(pl.multiple_of((1 - core) * half, half), half), :] = other_ref[...]


def norm_kernel(x_ref, normed_t_ref, normed_ref, gram_ref):
    xfloat = x_ref[...].astype(f32)
    mean = jnp.mean(xfloat * xfloat, axis=0, keepdims=True)
    scaled = (xfloat * lax.rsqrt(mean + 1e-06)).astype(bf16)
    normed_t_ref[...] = scaled
    flat = scaled.T
    normed_ref[...] = flat
    gram_ref[...] = mm_nt(flat, flat)


def first_kernel(
    core_ref, normed, own_ref, goal_ref, up_ref, down_ref,
    pre_ref, act_ref, keep_ref, send_ref,
    total, wide,
):
    j = pl.program_id(0)

    @pl.when(j == 0)
    def _():
        total[...] = place_gap(core_ref, own_ref, goal_ref, 0, wide)

    pre = mm(normed[...], up_ref[...])
    pre_ref[...] = pre
    act = gelu_parts(pre[:TOK])[0].astype(bf16)
    act_ref[...] = act
    total[...] += mm(act, down_ref[...])

    @pl.when(j == pl.num_programs(0) - 1)
    def _():
        hand_out(core_ref, total, keep_ref, send_ref)


def second_kernel(
    core_ref, mine_ref, other_ref, own_ref, goal_ref, down_ref, pre_ref, act_ref, gram_ref,
    resid_ref, resid_t_ref, dpre_ref, pre_2_ref, act_2_ref, keep_ref, send_ref,
    total, wide, cross,
):
    j = pl.program_id(0)

    @pl.when(j == 0)
    def _():
        take_in(core_ref, mine_ref, other_ref, resid_ref)
        total[...] = place_gap(core_ref, own_ref, goal_ref, 1, wide)
        cross[...] = jnp.zeros_like(cross)
        resid_t_ref[...] = resid_ref[...].T

    back = mm(down_ref[...], resid_t_ref[...]).T
    dpre = (back * gelu_parts(pre_ref[:TOK, :])[1]).astype(bf16)
    dpre_ref[...] = dpre
    pre_2 = pre_ref[TOK:, :] - local_rate * mm_split(gram_ref[TOK:, :TOK], dpre)
    pre_2_ref[...] = pre_2
    act_2 = gelu_parts(pre_2)[0].astype(bf16)
    act_2_ref[...] = act_2
    total[...] += mm(act_2, down_ref[...])
    cross[...] += mm_nt(act_2, act_ref[...])

    @pl.when(j == pl.num_programs(0) - 1)
    def _():
        total[...] -= local_rate * mm_split(cross[...], resid_ref[...])
        hand_out(core_ref, total, keep_ref, send_ref)


def third_kernel(
    core_ref, mine_ref, other_ref, resid_ref, down_ref, act_ref, act_2_ref, pre_2_ref, dpre_ref, gram_ref,
    resid_t_ref, dpre_2_ref, squared_ref,
    resid_2, gram_resid, gram_act, gram_dpre,
):
    j = pl.program_id(0)

    @pl.when(j == 0)
    def _():
        take_in(core_ref, mine_ref, other_ref, resid_2)
        both = jnp.concatenate([resid_ref[...], resid_2[...]], axis=0)
        gram_resid[...] = mm_nt(both, both)
        gram_act[...] = jnp.zeros_like(gram_act)
        gram_dpre[...] = jnp.zeros_like(gram_dpre)
        resid_t_ref[...] = resid_2[...].T

    back = mm(down_ref[...], resid_t_ref[...]).T - local_rate * mm_split(
        gram_resid[TOK:, :TOK], act_ref[...]
    )
    dpre_2 = (back * gelu_parts(pre_2_ref[...])[1]).astype(bf16)
    dpre_2_ref[...] = dpre_2
    acts = jnp.concatenate([act_ref[...], act_2_ref[...]], axis=0)
    gram_act[...] += mm_nt(acts, acts)
    dpres = jnp.concatenate([dpre_ref[...], dpre_2], axis=0)
    gram_dpre[...] += mm_nt(dpres, dpres)

    @pl.when(j == pl.num_programs(0) - 1)
    def _():
        terms = gram_ref[...] * gram_dpre[...] + gram_resid[...] * gram_act[...]
        squared_ref[...] = jnp.full((8, 128), (local_rate * local_rate) * jnp.sum(terms), f32)


def whole(shape):
    return pl.BlockSpec(shape, lambda j: (0,) * len(shape))


def columns(rows):
    return pl.BlockSpec((rows, PART), lambda j: (0, j))


DOWN_ROWS = pl.BlockSpec((PART, D), lambda j: (j, 0))
SCALAR = pl.BlockSpec(memory_space=pltpu.SMEM)
HALF_TOK = (TOK // 2, D)


def call(kernel, in_specs, out_specs, out_types, scratch, flops, moved):
    return pl.pallas_call(
        kernel,
        grid=(D // PART,),
        in_specs=in_specs,
        out_specs=out_specs,
        out_shape=[jax.ShapeDtypeStruct(*kind) for kind in out_types],
        scratch_shapes=[pltpu.VMEM(*kind) for kind in scratch],
        compiler_params=pltpu.CompilerParams(vmem_limit_bytes=57 * 1024 * 1024),
        cost_estimate=pl.CostEstimate(flops=flops, bytes_accessed=moved, transcendentals=0),
    )


def sum_kernel(*refs):
    bound = clip_rms * math.sqrt(2.0 * D * F)
    total = None
    for k in range(4):
        rows, cols_1, cols_2, squared = refs[4 * k : 4 * k + 4]
        cols = jnp.concatenate([cols_1[...], cols_2[...]], axis=0)
        size = jnp.sqrt(squared[0:1, 0:1])
        scale = -local_rate * (bound / jnp.maximum(size, bound))
        term = scale * mm(rows[...], cols)
        total = term if total is None else total + term
    refs[16][...] = total


def sum_clients(rows, cols_1, cols_2, squared):
    narrow = whole((D // 4, 2 * TOK))
    operands = []
    for k in range(4):
        operands += [rows[k], cols_1[k], cols_2[k], squared[k]]
    return call(
        sum_kernel,
        [narrow, columns(TOK), columns(TOK), whole((8, 128))] * 4,
        [columns(D // 4)],
        [((D // 4, D), f32)],
        [],
        4 * TOK * D * D, 8 * TOK * D,
    )(*operands)[0]


def reduce_over_tp(keep, send):
    got = lax.ppermute(send, "tp", CORE_SWAP).astype(f32)
    chip = (keep + got).astype(bf16)
    far = lax.ppermute(chip, "tp", FAR_SWAP)
    mine = ((chip.astype(f32) + far.astype(f32)) * (1.0 / TOK)).astype(bf16)
    return mine, lax.ppermute(mine, "tp", CORE_SWAP)


def ring(piece, axis, up, down, me, n, after_first=lambda first: first):
    far = n // 2
    opposite = piece((me + far) % n)
    from_down = lax.ppermute(opposite[..., :HALF].astype(bf16), axis, up)
    from_up = lax.ppermute(opposite[..., HALF:].astype(bf16), axis, down)
    from_down, from_up = after_first((from_down, from_up))
    for distance in range(far - 1, 0, -1):
        ahead = piece((me + distance) % n)
        behind = piece((me + n - distance) % n)
        if distance == far - 1:
            ahead = jnp.concatenate(
                [ahead[..., :HALF] + from_down.astype(f32), ahead[..., HALF:]], axis=-1
            )
            behind = jnp.concatenate(
                [behind[..., :HALF], behind[..., HALF:] + from_up.astype(f32)], axis=-1
            )
        else:
            ahead = ahead + from_down.astype(f32)
            behind = behind + from_up.astype(f32)
        from_down = lax.ppermute(ahead.astype(bf16), axis, up)
        from_up = lax.ppermute(behind.astype(bf16), axis, down)
    return piece(me) + from_down.astype(f32) + from_up.astype(f32)


def swap_y(block, y_lo):
    halves = block.reshape(2, BLOCK // 2, D)
    mine = jnp.where(y_lo == 0, halves[0], halves[1])
    other = jnp.where(y_lo == 0, halves[1], halves[0]).astype(bf16)
    return mine + lax.ppermute(other, "region", Y_SWAP).astype(f32)


def shards(hidden_in, target, up_weight, down_weight, noise_up, noise_down):
    tp = lax.axis_index("tp")
    client = lax.axis_index("client")
    region = lax.axis_index("region")
    z = region // 2
    y_lo = region % 2

    def direct(array):
        return [array] + [lax.ppermute(array, "client", X_BY[d]) for d in (1, 2, 3)]

    def slices(array):
        parts = array.reshape(4, D // 4, array.shape[-1])
        pick = [
            lax.dynamic_index_in_dim(parts, (client + d) % 4, 0, keepdims=False) for d in range(4)
        ]
        return [pick[0]] + [lax.ppermute(pick[d], "client", X_BY[d]) for d in (1, 2, 3)]

    own = jnp.swapaxes(hidden_in[0], 1, 2)
    goal = jnp.swapaxes(target[0], 1, 2)
    states = lax.all_gather(
        jnp.concatenate([own[0], own[1]], axis=1), "tp", axis=0, tiled=True
    )
    spot = tp.astype(jnp.int32).reshape(1)
    narrow = whole((2, D // 4, TOK))

    normed_t, normed, gram = pl.pallas_call(
        norm_kernel,
        out_shape=[
            jax.ShapeDtypeStruct((D, 2 * TOK), bf16),
            jax.ShapeDtypeStruct((2 * TOK, D), bf16),
            jax.ShapeDtypeStruct((2 * TOK, 2 * TOK), f32),
        ],
        compiler_params=pltpu.CompilerParams(vmem_limit_bytes=32 * 1024 * 1024),
    )(states)
    rows_up = slices(normed_t)
    pre, act_1, keep, send = call(
        first_kernel,
        [SCALAR, whole((2 * TOK, D)), narrow, narrow, columns(D), DOWN_ROWS],
        [columns(2 * TOK), columns(TOK), whole(HALF_TOK), whole(HALF_TOK)],
        [((2 * TOK, D), f32), ((TOK, D), bf16), (HALF_TOK, f32), (HALF_TOK, bf16)],
        [((TOK, D), f32), ((D, TOK), f32)],
        6 * TOK * D * D, 4 * D * D,
    )(spot, normed, own, goal, up_weight, down_weight)
    keep, send, rows_up = hold((keep, send, rows_up))
    cols_down_1 = direct(act_1)
    mine, other = reduce_over_tp(keep, send)

    resid_1, resid_t_1, dpre_1, pre_2, act_2, keep, send = call(
        second_kernel,
        [SCALAR, whole(HALF_TOK), whole(HALF_TOK), narrow, narrow, DOWN_ROWS, columns(2 * TOK), columns(TOK), whole((2 * TOK, 2 * TOK))],
        [whole((TOK, D)), whole((D, TOK)), columns(TOK), columns(TOK), columns(TOK), whole(HALF_TOK), whole(HALF_TOK)],
        [((TOK, D), bf16), ((D, TOK), bf16), ((TOK, D), bf16), ((TOK, D), f32), ((TOK, D), bf16), (HALF_TOK, f32), (HALF_TOK, bf16)],
        [((TOK, D), f32), ((D, TOK), f32), ((TOK, TOK), f32)],
        4 * TOK * D * D, 2 * D * D,
    )(spot, mine, other, own, goal, down_weight, pre, act_1, gram)
    keep, send, cols_down_1 = hold((keep, send, cols_down_1))
    act_ahead = lax.ppermute(act_2, "client", X_BY[1])
    act_behind = lax.ppermute(act_2, "client", X_BY[3])
    rows_down_1 = slices(resid_t_1)
    mine, other = reduce_over_tp(keep, send)
    mine, other, act_ahead, act_behind, rows_down_1 = hold((mine, other, act_ahead, act_behind, rows_down_1))
    act_far = lax.ppermute(act_behind, "client", X_BY[3])
    cols_down_2 = [act_2, act_ahead, act_far, act_behind]
    dpre_ahead = lax.ppermute(dpre_1, "client", X_BY[1])
    dpre_behind = lax.ppermute(dpre_1, "client", X_BY[3])

    resid_t_2, dpre_2, squared = call(
        third_kernel,
        [SCALAR, whole(HALF_TOK), whole(HALF_TOK), whole((TOK, D)), DOWN_ROWS, columns(TOK), columns(TOK), columns(TOK), columns(TOK), whole((2 * TOK, 2 * TOK))],
        [whole((D, TOK)), columns(TOK), whole((8, 128))],
        [((D, TOK), bf16), ((TOK, D), bf16), ((8, 128), f32)],
        [((TOK, D), bf16)] + [((2 * TOK, 2 * TOK), f32)] * 3,
        2 * TOK * D * D, 2 * D * D,
    )(spot, mine, other, resid_1, down_weight, act_1, act_2, pre_2, dpre_1, gram)
    rows_down_2 = slices(resid_t_2)
    squared = squared + lax.ppermute(squared, "tp", CORE_SWAP)
    squared = squared + lax.ppermute(squared, "tp", FAR_SWAP)
    squared, cols_down_2, dpre_ahead, dpre_behind = hold((squared, cols_down_2, dpre_ahead, dpre_behind))
    squared = direct(squared)
    squared, rows_down_2, dpre_2 = hold((squared, rows_down_2, dpre_2))
    dpre_far = lax.ppermute(dpre_ahead, "client", X_BY[1])
    cols_up_1 = [dpre_1, dpre_ahead, dpre_far, dpre_behind]
    late_ahead = lax.ppermute(dpre_2, "client", X_BY[1])
    late_behind = lax.ppermute(dpre_2, "client", X_BY[3])

    rows_down = [jnp.concatenate([a, b], axis=1) for a, b in zip(rows_down_1, rows_down_2)]
    down_x = sum_clients(rows_down, cols_down_1, cols_down_2, squared)
    def at(array):
        array = array.reshape(8, BLOCK, D)
        return lambda k: lax.dynamic_index_in_dim(array, k, 0, keepdims=False)

    late = (late_ahead, late_behind, cols_up_1)
    arrived = []

    def with_late(first):
        first, *rest = hold((first, *late))
        arrived.extend(rest)
        return first

    down_x = ring(at(down_x), "region", Z_UP, Z_DOWN, z, 8, with_late)
    late_ahead, late_behind, cols_up_1 = arrived
    top = lax.ppermute(late_ahead[: TOK // 2], "client", X_BY[1])
    bottom = lax.ppermute(late_behind[TOK // 2 :], "client", X_BY[3])
    cols_up_2 = [dpre_2, late_ahead, jnp.concatenate([top, bottom], axis=0), late_behind]
    up_x = sum_clients(rows_up, cols_up_1, cols_up_2, squared)
    up_z = ring(at(up_x), "region", Z_UP, Z_DOWN, z, 8)
    total_up = swap_y(up_z, y_lo)
    total_down = swap_y(down_x, y_lo).T

    count = 64
    rows = D // count
    block = client * 16 + region
    base_up = lax.dynamic_slice_in_dim(up_weight, block * rows, rows, 0).astype(f32)
    base_down = lax.dynamic_slice_in_dim(down_weight, block * rows, rows, 1).astype(f32)
    root = math.sqrt(count)
    scale = server_rate / (clip_rms * root)
    new_up = base_up + scale * (total_up + clip_rms * root * noise_up)
    new_down = base_down + scale * (total_down + clip_rms * root * noise_down)
    return (new_up, new_down)


def solution(mesh):
    placed = (
        P(("client", "region"), None, None, "tp"),
        P(("client", "region"), None, None, "tp"),
        P(None, "tp"),
        P("tp", None),
        P(("client", "region"), "tp"),
        P("tp", ("client", "region")),
    )
    return jax.shard_map(
        shards,
        mesh=mesh,
        in_specs=placed,
        out_specs=(P(("client", "region"), "tp"), P("tp", ("client", "region"))),
        check_vma=False,
    )
```

```python
import math

import jax
import jax.numpy as jnp
from jax import lax
from jax.experimental import pallas as pl
from jax.experimental.pallas import tpu as pltpu
from jax.sharding import PartitionSpec as P

D = 1792
F = 7168
TOK = 128
HALF = 896
BLOCK = 56
PART = 256
BLOCKS = D // PART
VMEM_BYTES = 48 * 1024 * 1024
ROOT_2_PI = math.sqrt(2.0 / math.pi)

local_rate = 0.5
clip_rms = 0.08
server_rate = 0.02

X_UP = [(i, (i + 1) % 4) for i in range(4)]
X_DOWN = [(i, (i + 3) % 4) for i in range(4)]
Z_UP = [(i, (i + 2) % 16) for i in range(16)]
Z_DOWN = [(i, (i + 14) % 16) for i in range(16)]
Y_SWAP = [(i, i ^ 1) for i in range(16)]
CORE_SWAP = [(i, i ^ 1) for i in range(4)]
FAR_SWAP = [(i, i ^ 2) for i in range(4)]

f32 = jnp.float32
bf16 = jnp.bfloat16
hold = lax.optimization_barrier


def mm(left, right):
    return jnp.dot(left, right, preferred_element_type=f32)


def mm_nt(left, right):
    return lax.dot_general(left, right, (((1,), (1,)), ((), ())), preferred_element_type=f32)


def mm_split(left, right):
    high = left.astype(bf16)
    low = (left - high.astype(f32)).astype(bf16)
    return mm(high, right) + mm(low, right)


def gelu_parts(pre):
    square = pre * pre
    curve = jnp.tanh(ROOT_2_PI * (pre + 0.044715 * pre * square))
    value = 0.5 * pre * (1.0 + curve)
    slope = 0.5 * (1.0 + curve) + 0.5 * pre * (1.0 - curve * curve) * (
        ROOT_2_PI * (1.0 + 3.0 * 0.044715 * square)
    )
    return value, slope


def place_gap(core_ref, own_ref, goal_ref, step, wide):
    wide[...] = jnp.zeros_like(wide)
    start = pl.multiple_of(core_ref[0] * (D // 4), 64)
    wide[pl.ds(start, D // 4), :] = own_ref[step].astype(f32) - goal_ref[step].astype(f32)
    return wide[...].T


def hand_out(core_ref, total, keep_ref, send_ref):
    core = core_ref[0] % 2
    half = TOK // 2
    keep_ref[...] = total[pl.ds(pl.multiple_of(core * half, half), half), :]
    other = total[pl.ds(pl.multiple_of((1 - core) * half, half), half), :]
    send_ref[...] = other.astype(bf16)


def take_in(core_ref, mine_ref, other_ref, resid):
    core = core_ref[0] % 2
    half = TOK // 2
    resid[pl.ds(pl.multiple_of(core * half, half), half), :] = mine_ref[...]
    resid[pl.ds(pl.multiple_of((1 - core) * half, half), half), :] = other_ref[...]


def norm_kernel(x_ref, normed_t_ref, normed_ref, gram_ref):
    xfloat = x_ref[...].astype(f32)
    mean = jnp.mean(xfloat * xfloat, axis=0, keepdims=True)
    scaled = (xfloat * lax.rsqrt(mean + 1e-06)).astype(bf16)
    normed_t_ref[...] = scaled
    flat = scaled.T
    normed_ref[...] = flat
    gram_ref[...] = mm_nt(flat, flat)


def first_kernel(
    j, core_ref, normed, own_ref, goal_ref, up_ref, down_ref,
    pre_ref, act_ref, keep_ref, send_ref,
    total, wide,
):
    @pl.when(j == 0)
    def _():
        total[...] = place_gap(core_ref, own_ref, goal_ref, 0, wide)

    pre = mm(normed[...], up_ref[...])
    pre_ref[...] = pre
    act = gelu_parts(pre[:TOK])[0].astype(bf16)
    act_ref[...] = act
    total[...] += mm(act, down_ref[...])

    @pl.when(j == BLOCKS - 1)
    def _():
        hand_out(core_ref, total, keep_ref, send_ref)


def second_kernel(
    j, core_ref, mine_ref, other_ref, own_ref, goal_ref, down_ref, pre_ref, act_ref, gram_ref,
    resid_ref, resid_t_ref, dpre_ref, pre_2_ref, act_2_ref, keep_ref, send_ref,
    total, wide, cross,
):

    @pl.when(j == 0)
    def _():
        take_in(core_ref, mine_ref, other_ref, resid_ref)
        total[...] = place_gap(core_ref, own_ref, goal_ref, 1, wide)
        cross[...] = jnp.zeros_like(cross)
        resid_t_ref[...] = resid_ref[...].T

    back = mm_nt(resid_ref[...], down_ref[...])
    dpre = (back * gelu_parts(pre_ref[:TOK, :])[1]).astype(bf16)
    dpre_ref[...] = dpre
    pre_2 = pre_ref[TOK:, :] - local_rate * mm_split(gram_ref[TOK:, :TOK], dpre)
    pre_2_ref[...] = pre_2
    act_2 = gelu_parts(pre_2)[0].astype(bf16)
    act_2_ref[...] = act_2
    total[...] += mm(act_2, down_ref[...])
    cross[...] += mm_nt(act_2, act_ref[...])

    @pl.when(j == BLOCKS - 1)
    def _():
        total[...] -= local_rate * mm_split(cross[...], resid_ref[...])
        hand_out(core_ref, total, keep_ref, send_ref)


def third_kernel(
    j, core_ref, mine_ref, other_ref, resid_ref, down_ref, act_ref, act_2_ref, pre_2_ref, dpre_ref, gram_ref,
    resid_t_ref, dpre_2_ref, squared_ref,
    resid_2, gram_resid, gram_act, gram_dpre,
):

    @pl.when(j == 0)
    def _():
        take_in(core_ref, mine_ref, other_ref, resid_2)
        both = jnp.concatenate([resid_ref[...], resid_2[...]], axis=0)
        gram_resid[...] = mm_nt(both, both)
        gram_act[...] = jnp.zeros_like(gram_act)
        gram_dpre[...] = jnp.zeros_like(gram_dpre)
        resid_t_ref[...] = resid_2[...].T

    back = mm_nt(resid_2[...], down_ref[...]) - local_rate * mm_split(
        gram_resid[TOK:, :TOK], act_ref[...]
    )
    dpre_2 = (back * gelu_parts(pre_2_ref[...])[1]).astype(bf16)
    dpre_2_ref[...] = dpre_2
    acts = jnp.concatenate([act_ref[...], act_2_ref[...]], axis=0)
    gram_act[...] += mm_nt(acts, acts)
    dpres = jnp.concatenate([dpre_ref[...], dpre_2], axis=0)
    gram_dpre[...] += mm_nt(dpres, dpres)

    @pl.when(j == BLOCKS - 1)
    def _():
        terms = gram_ref[...] * gram_dpre[...] + gram_resid[...] * gram_act[...]
        squared_ref[...] = jnp.full((8, 128), (local_rate * local_rate) * jnp.sum(terms), f32)


def whole(ref, j):
    return ref


def columns(ref, j):
    return ref.at[:, pl.ds(j * PART, PART)]


def rows(ref, j):
    return ref.at[pl.ds(j * PART, PART), :]


def weight_columns(ref, j):
    return columns(ref, j)


def weight_rows(ref, j):
    return rows(ref, j)


HALF_TOK = (TOK // 2, D)


def call(kernel, views, out_types, scratch, flops, moved):
    weights = [i for i, view in enumerate(views) if view in (weight_rows, weight_columns)]
    ahead = 3

    def body(*refs):
        own = refs[len(views) : len(views) + len(scratch)]
        held = refs[len(views) + len(scratch) :]
        copies = {}

        def start(j):
            for n, i in enumerate(weights):
                copies[n, j] = pltpu.make_async_copy(
                    views[i](refs[i], j), views[i](held[2 * n], j), held[2 * n + 1].at[j]
                )
                copies[n, j].start()

        for j in range(ahead):
            start(j)
        for j in range(BLOCKS):
            if j + ahead < BLOCKS:
                start(j + ahead)
            seen = []
            for i, view in enumerate(views):
                if i in weights:
                    copies[weights.index(i), j].wait()
                    seen.append(view(held[2 * weights.index(i)], j))
                else:
                    seen.append(view(refs[i], j))
            kernel(j, *seen, *own)

    vmem = pl.BlockSpec(memory_space=pltpu.VMEM)
    smem = pl.BlockSpec(memory_space=pltpu.SMEM)
    return pl.pallas_call(
        body,
        in_specs=[smem]
        + [
            pl.BlockSpec(memory_space=pl.ANY) if i in weights else vmem
            for i in range(1, len(views) - len(out_types))
        ],
        out_specs=[vmem] * len(out_types),
        out_shape=[jax.ShapeDtypeStruct(*kind) for kind in out_types],
        scratch_shapes=[pltpu.VMEM(*kind) for kind in scratch]
        + [pltpu.VMEM((D, D), bf16), pltpu.SemaphoreType.DMA((BLOCKS,))] * len(weights),
        compiler_params=pltpu.CompilerParams(vmem_limit_bytes=VMEM_BYTES),
        cost_estimate=pl.CostEstimate(flops=flops, bytes_accessed=moved, transcendentals=0),
    )


def reduce_over_tp(keep, send):
    got = lax.ppermute(send, "tp", CORE_SWAP).astype(f32)
    chip = (keep + got).astype(bf16)
    far = lax.ppermute(chip, "tp", FAR_SWAP)
    mine = ((chip.astype(f32) + far.astype(f32)) * (1.0 / TOK)).astype(bf16)
    return mine, lax.ppermute(mine, "tp", CORE_SWAP)


def ring(piece, axis, up, down, me, n):
    far = n // 2
    opposite = piece((me + far) % n).astype(bf16)
    got = (
        lax.ppermute(opposite[..., :HALF], axis, up),
        lax.ppermute(opposite[..., HALF:], axis, down),
    )
    for distance in range(far - 1, 0, -1):
        got = yield got
        from_down, from_up = [array.astype(f32) for array in got]
        ahead = piece((me + distance) % n)
        behind = piece((me + n - distance) % n)
        if distance == far - 1:
            ahead = jnp.concatenate(
                [ahead[..., :HALF] + from_down, ahead[..., HALF:]], axis=-1
            )
            behind = jnp.concatenate(
                [behind[..., :HALF], behind[..., HALF:] + from_up], axis=-1
            )
        else:
            ahead = ahead + from_down
            behind = behind + from_up
        ahead, behind = yield (ahead.astype(bf16), behind.astype(bf16))
        got = (lax.ppermute(ahead, axis, up), lax.ppermute(behind, axis, down))
    got = yield got
    return piece(me) + got[0].astype(f32) + got[1].astype(f32)


def finish(steps, pair):
    try:
        while True:
            pair = steps.send(hold(pair))
    except StopIteration as end:
        return end.value


def swap_y(block, y_lo):
    halves = block.reshape(2, BLOCK // 2, D)
    mine = jnp.where(y_lo == 0, halves[0], halves[1])
    other = jnp.where(y_lo == 0, halves[1], halves[0]).astype(bf16)
    return mine + lax.ppermute(other, "region", Y_SWAP).astype(f32)


def shards(hidden_in, target, up_weight, down_weight, noise_up, noise_down):
    tp = lax.axis_index("tp")
    client = lax.axis_index("client")
    region = lax.axis_index("region")
    z = region // 2
    y_lo = region % 2

    own = jnp.swapaxes(hidden_in[0], 1, 2)
    goal = jnp.swapaxes(target[0], 1, 2)
    states = lax.all_gather(
        jnp.concatenate([own[0], own[1]], axis=1), "tp", axis=0, tiled=True
    )
    spot = tp.astype(jnp.int32).reshape(1)

    normed_t, normed, gram = pl.pallas_call(
        norm_kernel,
        out_shape=[
            jax.ShapeDtypeStruct((D, 2 * TOK), bf16),
            jax.ShapeDtypeStruct((2 * TOK, D), bf16),
            jax.ShapeDtypeStruct((2 * TOK, 2 * TOK), f32),
        ],
        compiler_params=pltpu.CompilerParams(vmem_limit_bytes=VMEM_BYTES),
    )(states)
    pre, act_1, keep, send = call(
        first_kernel,
        [whole, whole, whole, whole, weight_columns, weight_rows] + [columns, columns, whole, whole],
        [((2 * TOK, D), f32), ((TOK, D), bf16), (HALF_TOK, f32), (HALF_TOK, bf16)],
        [((TOK, D), f32), ((D, TOK), f32)],
        6 * TOK * D * D, 4 * D * D,
    )(spot, normed, own, goal, up_weight, down_weight)
    mine, other = reduce_over_tp(keep, send)

    resid_1, resid_t_1, dpre_1, pre_2, act_2, keep, send = call(
        second_kernel,
        [whole, whole, whole, whole, whole, weight_rows, columns, columns, whole]
        + [whole, whole, columns, columns, columns, whole, whole],
        [((TOK, D), bf16), ((D, TOK), bf16), ((TOK, D), bf16), ((TOK, D), f32), ((TOK, D), bf16), (HALF_TOK, f32), (HALF_TOK, bf16)],
        [((TOK, D), f32), ((D, TOK), f32), ((TOK, TOK), f32)],
        4 * TOK * D * D, 2 * D * D,
    )(spot, mine, other, own, goal, down_weight, pre, act_1, gram)
    mine, other = reduce_over_tp(keep, send)

    resid_t_2, dpre_2, squared = call(
        third_kernel,
        [whole, whole, whole, whole, weight_rows, columns, columns, columns, columns, whole]
        + [whole, columns, whole],
        [((D, TOK), bf16), ((TOK, D), bf16), ((8, 128), f32)],
        [((TOK, D), bf16)] + [((2 * TOK, 2 * TOK), f32)] * 3,
        2 * TOK * D * D, 2 * D * D,
    )(spot, mine, other, resid_1, down_weight, act_1, act_2, pre_2, dpre_1, gram)
    acts = jnp.concatenate([act_1, act_2], axis=0)
    dpres = jnp.concatenate([dpre_1, dpre_2], axis=0)
    resids_t = jnp.concatenate([resid_t_1, resid_t_2], axis=1)

    squared = squared + lax.ppermute(squared, "tp", CORE_SWAP)
    squared = squared + lax.ppermute(squared, "tp", FAR_SWAP)
    squared = squared[0, 0]
    bound = clip_rms * math.sqrt(2.0 * D * F)
    factor = bound / jnp.maximum(jnp.sqrt(squared), bound)
    scale_own = -local_rate * factor

    rows_up = normed_t.reshape(4, 8, BLOCK, 2 * TOK)
    rows_down = resids_t.reshape(4, 8, BLOCK, 2 * TOK)

    def up_piece(k):
        rows = lax.dynamic_index_in_dim(rows_up, k, 0, keepdims=False)
        return scale_own * mm(rows.reshape(8 * BLOCK, 2 * TOK), dpres)

    def down_piece(k):
        rows = lax.dynamic_index_in_dim(rows_down, k, 1, keepdims=False)
        return scale_own * mm(rows.reshape(4 * BLOCK, 2 * TOK), acts)

    along_z = ring(down_piece, "region", Z_UP, Z_DOWN, z, 8)
    along_x = ring(up_piece, "client", X_UP, X_DOWN, client, 4)
    leaving = along_z.send(hold(next(along_z)))
    arrived = hold((next(along_x), leaving))[0]
    down_z = finish(along_z, leaving)
    up_x = finish(along_x, along_x.send(arrived))
    up_x = up_x.reshape(8, BLOCK, D)
    down_z = down_z.reshape(4, BLOCK, D)

    def at(array):
        return lambda k: lax.dynamic_index_in_dim(array, k, 0, keepdims=False)

    along_z = ring(at(up_x), "region", Z_UP, Z_DOWN, z, 8)
    along_x = ring(at(down_z), "client", X_UP, X_DOWN, client, 4)
    up_z = finish(along_z, next(along_z))
    down_x = finish(along_x, next(along_x))
    total_up = swap_y(up_z, y_lo)
    total_down = swap_y(down_x, y_lo).T

    count = 64
    width = D // count
    block = client * 16 + region
    base_up = lax.dynamic_slice_in_dim(up_weight, block * width, width, 0).astype(f32)
    base_down = lax.dynamic_slice_in_dim(down_weight, block * width, width, 1).astype(f32)
    root = math.sqrt(count)
    scale = server_rate / (clip_rms * root)
    new_up = base_up + scale * (total_up + clip_rms * root * noise_up)
    new_down = base_down + scale * (total_down + clip_rms * root * noise_down)
    return (new_up, new_down)


def solution(mesh):
    placed = (
        P(("client", "region"), None, None, "tp"),
        P(("client", "region"), None, None, "tp"),
        P(None, "tp"),
        P("tp", None),
        P(("client", "region"), "tp"),
        P("tp", ("client", "region")),
    )
    return jax.shard_map(
        shards,
        mesh=mesh,
        in_specs=placed,
        out_specs=(P(("client", "region"), "tp"), P("tp", ("client", "region"))),
        check_vma=False,
    )
```

```python
import math

import jax
import jax.numpy as jnp
from jax import lax
from jax.experimental import pallas as pl
from jax.experimental.pallas import tpu as pltpu
from jax.sharding import PartitionSpec as P

D = 1792
F = 7168
TOK = 128
HALF = 896
BLOCK = 56
PART = 256
BLOCKS = D // PART
VMEM_BYTES = 48 * 1024 * 1024
ROOT_2_PI = math.sqrt(2.0 / math.pi)

local_rate = 0.5
clip_rms = 0.08
server_rate = 0.02

X_UP = [(i, (i + 1) % 4) for i in range(4)]
X_DOWN = [(i, (i + 3) % 4) for i in range(4)]
Z_UP = [(i, (i + 2) % 16) for i in range(16)]
Z_DOWN = [(i, (i + 14) % 16) for i in range(16)]
Y_SWAP = [(i, i ^ 1) for i in range(16)]
CORE_SWAP = [(i, i ^ 1) for i in range(4)]
FAR_SWAP = [(i, i ^ 2) for i in range(4)]

f32 = jnp.float32
bf16 = jnp.bfloat16
hold = lax.optimization_barrier


def mm(left, right):
    return jnp.dot(left, right, preferred_element_type=f32)


def mm_nt(left, right):
    return lax.dot_general(left, right, (((1,), (1,)), ((), ())), preferred_element_type=f32)


def mm_split(left, right):
    high = left.astype(bf16)
    low = (left - high.astype(f32)).astype(bf16)
    return mm(high, right) + mm(low, right)


def gelu_parts(pre):
    square = pre * pre
    curve = jnp.tanh(ROOT_2_PI * (pre + 0.044715 * pre * square))
    value = 0.5 * pre * (1.0 + curve)
    slope = 0.5 * (1.0 + curve) + 0.5 * pre * (1.0 - curve * curve) * (
        ROOT_2_PI * (1.0 + 3.0 * 0.044715 * square)
    )
    return value, slope


def place_gap(core_ref, own_ref, goal_ref, step, wide):
    wide[...] = jnp.zeros_like(wide)
    start = pl.multiple_of(core_ref[0] * (D // 4), 64)
    wide[pl.ds(start, D // 4), :] = own_ref[step].astype(f32) - goal_ref[step].astype(f32)
    return wide[...].T


def hand_out(core_ref, total, keep_ref, send_ref):
    core = core_ref[0] % 2
    half = TOK // 2
    keep_ref[...] = total[pl.ds(pl.multiple_of(core * half, half), half), :]
    other = total[pl.ds(pl.multiple_of((1 - core) * half, half), half), :]
    send_ref[...] = other.astype(bf16)


def take_in(core_ref, mine_ref, other_ref, resid):
    core = core_ref[0] % 2
    half = TOK // 2
    resid[pl.ds(pl.multiple_of(core * half, half), half), :] = mine_ref[...]
    resid[pl.ds(pl.multiple_of((1 - core) * half, half), half), :] = other_ref[...]


def norm_kernel(x_ref, normed_t_ref, normed_ref, gram_ref):
    xfloat = x_ref[...].astype(f32)
    mean = jnp.mean(xfloat * xfloat, axis=0, keepdims=True)
    scaled = (xfloat * lax.rsqrt(mean + 1e-06)).astype(bf16)
    normed_t_ref[...] = scaled
    flat = scaled.T
    normed_ref[...] = flat
    gram_ref[...] = mm_nt(flat, flat)


def block(j):
    return pl.ds(j * PART, PART)


def first_kernel(
    wait, core_ref, normed, own_ref, goal_ref, up_ref, down_ref,
    pre_ref, act_ref, keep_ref, send_ref,
    total, wide,
):
    total[...] = place_gap(core_ref, own_ref, goal_ref, 0, wide)
    for j in range(BLOCKS):
        wait(0, j)
        pre = mm(normed[...], up_ref[:, block(j)])
        pre_ref[:, block(j)] = pre
        act_ref[:, block(j)] = gelu_parts(pre[:TOK])[0].astype(bf16)
    for j in range(BLOCKS):
        wait(1, j)
    for j in range(BLOCKS):
        total[:, block(j)] += mm(act_ref[...], down_ref[:, block(j)])
    hand_out(core_ref, total, keep_ref, send_ref)


def second_kernel(
    wait, core_ref, mine_ref, other_ref, own_ref, goal_ref, down_ref, pre_ref, act_ref, gram_ref,
    resid_ref, resid_t_ref, dpre_ref, pre_2_ref, act_2_ref, keep_ref, send_ref,
    total, wide,
):
    take_in(core_ref, mine_ref, other_ref, resid_ref)
    for j in range(BLOCKS):
        wait(0, j)
        back = mm_nt(resid_ref[...], down_ref[block(j), :])
        dpre_ref[:, block(j)] = (back * gelu_parts(pre_ref[:TOK, block(j)])[1]).astype(bf16)
    for j in range(BLOCKS):
        pre_2 = pre_ref[TOK:, block(j)] - local_rate * mm_split(
            gram_ref[TOK:, :TOK], dpre_ref[:, block(j)]
        )
        pre_2_ref[:, block(j)] = pre_2
        act_2_ref[:, block(j)] = gelu_parts(pre_2)[0].astype(bf16)
    total[...] = place_gap(core_ref, own_ref, goal_ref, 1, wide)
    cross = mm_nt(act_2_ref[...], act_ref[...])
    for j in range(BLOCKS):
        total[:, block(j)] += mm(act_2_ref[...], down_ref[:, block(j)]) - local_rate * mm_split(
            cross, resid_ref[:, block(j)]
        )
    hand_out(core_ref, total, keep_ref, send_ref)
    resid_t_ref[...] = resid_ref[...].T


def third_kernel(
    wait, core_ref, mine_ref, other_ref, resid_ref, down_ref, act_ref, act_2_ref, pre_2_ref, dpre_ref, gram_ref,
    resid_t_ref, dpre_2_ref, squared_ref,
    resid_2,
):
    take_in(core_ref, mine_ref, other_ref, resid_2)
    both = jnp.concatenate([resid_ref[...], resid_2[...]], axis=0)
    gram_resid = mm_nt(both, both)
    for j in range(BLOCKS):
        wait(0, j)
        back = mm_nt(resid_2[...], down_ref[block(j), :]) - local_rate * mm_split(
            gram_resid[TOK:, :TOK], act_ref[:, block(j)]
        )
        dpre_2_ref[:, block(j)] = (back * gelu_parts(pre_2_ref[:, block(j)])[1]).astype(bf16)
    acts = jnp.concatenate([act_ref[...], act_2_ref[...]], axis=0)
    dpres = jnp.concatenate([dpre_ref[...], dpre_2_ref[...]], axis=0)
    terms = gram_ref[...] * mm_nt(dpres, dpres) + gram_resid * mm_nt(acts, acts)
    squared_ref[...] = jnp.full((8, 128), (local_rate * local_rate) * jnp.sum(terms), f32)
    resid_t_ref[...] = resid_2[...].T


def whole(ref, j):
    return ref


def columns(ref, j):
    return ref.at[:, pl.ds(j * PART, PART)]


def rows(ref, j):
    return ref.at[pl.ds(j * PART, PART), :]


def weight_columns(ref, j):
    return columns(ref, j)


def weight_rows(ref, j):
    return rows(ref, j)


HALF_TOK = (TOK // 2, D)


def call(kernel, views, out_types, scratch, flops, moved):
    weights = [i for i, view in enumerate(views) if view in (weight_rows, weight_columns)]
    def body(*refs):
        refs = list(refs)
        own = refs[len(views) : len(views) + len(scratch)]
        held = refs[len(views) + len(scratch) :]
        copies = {}
        for n, i in enumerate(weights):
            for j in range(BLOCKS):
                copies[n, j] = pltpu.make_async_copy(
                    views[i](refs[i], j), views[i](held[2 * n], j), held[2 * n + 1].at[j]
                )
                copies[n, j].start()
            refs[i] = held[2 * n]
        kernel(lambda n, j: copies[n, j].wait(), *refs[: len(views)], *own)

    vmem = pl.BlockSpec(memory_space=pltpu.VMEM)
    smem = pl.BlockSpec(memory_space=pltpu.SMEM)
    return pl.pallas_call(
        body,
        in_specs=[smem]
        + [
            pl.BlockSpec(memory_space=pl.ANY) if i in weights else vmem
            for i in range(1, len(views) - len(out_types))
        ],
        out_specs=[vmem] * len(out_types),
        out_shape=[jax.ShapeDtypeStruct(*kind) for kind in out_types],
        scratch_shapes=[pltpu.VMEM(*kind) for kind in scratch]
        + [pltpu.VMEM((D, D), bf16), pltpu.SemaphoreType.DMA((BLOCKS,))] * len(weights),
        compiler_params=pltpu.CompilerParams(vmem_limit_bytes=VMEM_BYTES),
        cost_estimate=pl.CostEstimate(flops=flops, bytes_accessed=moved, transcendentals=0),
    )


def reduce_over_tp(keep, send):
    got = lax.ppermute(send, "tp", CORE_SWAP).astype(f32)
    chip = (keep + got).astype(bf16)
    far = lax.ppermute(chip, "tp", FAR_SWAP)
    mine = ((chip.astype(f32) + far.astype(f32)) * (1.0 / TOK)).astype(bf16)
    return mine, lax.ppermute(mine, "tp", CORE_SWAP)


def ring(piece, axis, up, down, me, n, farthest=None):
    far = n // 2
    opposite = (farthest or piece)((me + far) % n).astype(bf16)
    got = (
        lax.ppermute(opposite[..., :HALF], axis, up),
        lax.ppermute(opposite[..., HALF:], axis, down),
    )
    for distance in range(far - 1, 0, -1):
        got = yield got
        from_down, from_up = [array.astype(f32) for array in got]
        ahead = piece((me + distance) % n)
        behind = piece((me + n - distance) % n)
        if distance == far - 1:
            ahead = jnp.concatenate(
                [ahead[..., :HALF] + from_down, ahead[..., HALF:]], axis=-1
            )
            behind = jnp.concatenate(
                [behind[..., :HALF], behind[..., HALF:] + from_up], axis=-1
            )
        else:
            ahead = ahead + from_down
            behind = behind + from_up
        ahead, behind = yield (ahead.astype(bf16), behind.astype(bf16))
        got = (lax.ppermute(ahead, axis, up), lax.ppermute(behind, axis, down))
    got = yield got
    return piece(me) + got[0].astype(f32) + got[1].astype(f32)


def finish(steps, pair):
    try:
        while True:
            pair = steps.send(hold(pair))
    except StopIteration as end:
        return end.value


def swap_y(block, y_lo):
    halves = block.reshape(2, BLOCK // 2, D)
    mine = jnp.where(y_lo == 0, halves[0], halves[1])
    other = jnp.where(y_lo == 0, halves[1], halves[0]).astype(bf16)
    return mine + lax.ppermute(other, "region", Y_SWAP).astype(f32)


def shards(hidden_in, target, up_weight, down_weight, noise_up, noise_down):
    tp = lax.axis_index("tp")
    client = lax.axis_index("client")
    region = lax.axis_index("region")
    z = region // 2
    y_lo = region % 2

    own = jnp.swapaxes(hidden_in[0], 1, 2)
    goal = jnp.swapaxes(target[0], 1, 2)
    states = lax.all_gather(
        jnp.concatenate([own[0], own[1]], axis=1), "tp", axis=0, tiled=True
    )
    spot = tp.astype(jnp.int32).reshape(1)

    normed_t, normed, gram = pl.pallas_call(
        norm_kernel,
        out_shape=[
            jax.ShapeDtypeStruct((D, 2 * TOK), bf16),
            jax.ShapeDtypeStruct((2 * TOK, D), bf16),
            jax.ShapeDtypeStruct((2 * TOK, 2 * TOK), f32),
        ],
        compiler_params=pltpu.CompilerParams(vmem_limit_bytes=VMEM_BYTES),
    )(states)
    pre, act_1, keep, send = call(
        first_kernel,
        [whole, whole, whole, whole, weight_columns, weight_rows] + [columns, columns, whole, whole],
        [((2 * TOK, D), f32), ((TOK, D), bf16), (HALF_TOK, f32), (HALF_TOK, bf16)],
        [((TOK, D), f32), ((D, TOK), f32)],
        6 * TOK * D * D, 4 * D * D,
    )(spot, normed, own, goal, up_weight, down_weight)
    mine, other = reduce_over_tp(keep, send)

    resid_1, resid_t_1, dpre_1, pre_2, act_2, keep, send = call(
        second_kernel,
        [whole, whole, whole, whole, whole, weight_rows, columns, columns, whole]
        + [whole, whole, columns, columns, columns, whole, whole],
        [((TOK, D), bf16), ((D, TOK), bf16), ((TOK, D), bf16), ((TOK, D), f32), ((TOK, D), bf16), (HALF_TOK, f32), (HALF_TOK, bf16)],
        [((TOK, D), f32), ((D, TOK), f32)],
        4 * TOK * D * D, 2 * D * D,
    )(spot, mine, other, own, goal, down_weight, pre, act_1, gram)
    mine, other = reduce_over_tp(keep, send)

    resid_t_2, dpre_2, squared = call(
        third_kernel,
        [whole, whole, whole, whole, weight_rows, columns, columns, columns, columns, whole]
        + [whole, columns, whole],
        [((D, TOK), bf16), ((TOK, D), bf16), ((8, 128), f32)],
        [((TOK, D), bf16)],
        2 * TOK * D * D, 2 * D * D,
    )(spot, mine, other, resid_1, down_weight, act_1, act_2, pre_2, dpre_1, gram)
    acts = jnp.concatenate([act_1, act_2], axis=0)
    dpres = jnp.concatenate([dpre_1, dpre_2], axis=0)
    resids_t = jnp.concatenate([resid_t_1, resid_t_2], axis=1)

    rows_up = normed_t.reshape(4, 8, BLOCK, 2 * TOK)
    rows_down = resids_t.reshape(4, 8, BLOCK, 2 * TOK)

    def up_raw(k):
        picked = lax.dynamic_index_in_dim(rows_up, k, 0, keepdims=False)
        return -local_rate * mm(picked.reshape(8 * BLOCK, 2 * TOK), dpres)

    def up_piece(k):
        return factor * up_raw(k)

    def down_piece(k):
        picked = lax.dynamic_index_in_dim(rows_down, k, 1, keepdims=False)
        return (-local_rate * factor) * mm(picked.reshape(4 * BLOCK, 2 * TOK), acts)

    along_x = ring(up_piece, "client", X_UP, X_DOWN, client, 4, up_raw)
    arriving = next(along_x)

    squared = squared + lax.ppermute(squared, "tp", CORE_SWAP)
    squared = squared + lax.ppermute(squared, "tp", FAR_SWAP)
    bound = clip_rms * math.sqrt(2.0 * D * F)
    factors = bound / jnp.maximum(jnp.sqrt(squared), bound)
    factor = factors[0, 0]
    along_z = ring(down_piece, "region", Z_UP, Z_DOWN, z, 8)
    arriving_z = next(along_z)
    factor_below = lax.ppermute(factors, "client", X_UP)[0, 0]
    factor_above = lax.ppermute(factors, "client", X_DOWN)[0, 0]
    leaving = along_z.send(hold(arriving_z))
    arrived = hold((arriving, leaving))[0]
    arrived = (arrived[0].astype(f32) * factor_below, arrived[1].astype(f32) * factor_above)
    down_z = finish(along_z, leaving)
    up_x = finish(along_x, along_x.send(arrived))
    up_x = up_x.reshape(8, BLOCK, D)
    down_z = down_z.reshape(4, BLOCK, D)

    def at(array):
        return lambda k: lax.dynamic_index_in_dim(array, k, 0, keepdims=False)

    along_z = ring(at(up_x), "region", Z_UP, Z_DOWN, z, 8)
    along_x = ring(at(down_z), "client", X_UP, X_DOWN, client, 4)
    up_z = finish(along_z, next(along_z))
    down_x = finish(along_x, next(along_x))
    total_up = swap_y(up_z, y_lo)
    total_down = swap_y(down_x, y_lo).T

    count = 64
    width = D // count
    block = client * 16 + region
    base_up = lax.dynamic_slice_in_dim(up_weight, block * width, width, 0).astype(f32)
    base_down = lax.dynamic_slice_in_dim(down_weight, block * width, width, 1).astype(f32)
    root = math.sqrt(count)
    scale = server_rate / (clip_rms * root)
    new_up = base_up + scale * (total_up + clip_rms * root * noise_up)
    new_down = base_down + scale * (total_down + clip_rms * root * noise_down)
    return (new_up, new_down)


def solution(mesh):
    placed = (
        P(("client", "region"), None, None, "tp"),
        P(("client", "region"), None, None, "tp"),
        P(None, "tp"),
        P("tp", None),
        P(("client", "region"), "tp"),
        P("tp", ("client", "region")),
    )
    return jax.shard_map(
        shards,
        mesh=mesh,
        in_specs=placed,
        out_specs=(P(("client", "region"), "tp"), P("tp", ("client", "region"))),
        check_vma=False,
    )
```

```python
import math

import jax
import jax.numpy as jnp
from jax import lax
from jax.experimental import pallas as pl
from jax.experimental.pallas import tpu as pltpu
from jax.sharding import PartitionSpec as P

D = 1792
F = 7168
TOK = 128
HALF = 896
BLOCK = 56
PART = 256
BLOCKS = D // PART
VMEM_BYTES = 48 * 1024 * 1024
ROOT_2_PI = math.sqrt(2.0 / math.pi)

local_rate = 0.5
clip_rms = 0.08
server_rate = 0.02

X_UP = [(i, (i + 1) % 4) for i in range(4)]
X_DOWN = [(i, (i + 3) % 4) for i in range(4)]
Z_UP = [(i, (i + 2) % 16) for i in range(16)]
Z_DOWN = [(i, (i + 14) % 16) for i in range(16)]
Y_SWAP = [(i, i ^ 1) for i in range(16)]
CORE_SWAP = [(i, i ^ 1) for i in range(4)]
FAR_SWAP = [(i, i ^ 2) for i in range(4)]

f32 = jnp.float32
bf16 = jnp.bfloat16
hold = lax.optimization_barrier


def mm(left, right):
    return jnp.dot(left, right, preferred_element_type=f32)


def mm_nt(left, right):
    return lax.dot_general(left, right, (((1,), (1,)), ((), ())), preferred_element_type=f32)


def mm_split(left, right):
    high = left.astype(bf16)
    low = (left - high.astype(f32)).astype(bf16)
    return mm(high, right) + mm(low, right)


def gelu_parts(pre):
    square = pre * pre
    curve = jnp.tanh(ROOT_2_PI * (pre + 0.044715 * pre * square))
    value = 0.5 * pre * (1.0 + curve)
    slope = 0.5 * (1.0 + curve) + 0.5 * pre * (1.0 - curve * curve) * (
        ROOT_2_PI * (1.0 + 3.0 * 0.044715 * square)
    )
    return value, slope


def place_gap(core_ref, own_ref, goal_ref, step, wide):
    wide[...] = jnp.zeros_like(wide)
    start = pl.multiple_of(core_ref[0] * (D // 4), 64)
    wide[pl.ds(start, D // 4), :] = own_ref[step].astype(f32) - goal_ref[step].astype(f32)
    return wide[...].T


def hand_out(core_ref, total, keep_ref, send_ref):
    core = core_ref[0] % 2
    half = TOK // 2
    keep_ref[...] = total[pl.ds(pl.multiple_of(core * half, half), half), :]
    other = total[pl.ds(pl.multiple_of((1 - core) * half, half), half), :]
    send_ref[...] = other.astype(bf16)


def take_in(core_ref, mine_ref, other_ref, resid):
    core = core_ref[0] % 2
    half = TOK // 2
    resid[pl.ds(pl.multiple_of(core * half, half), half), :] = mine_ref[...]
    resid[pl.ds(pl.multiple_of((1 - core) * half, half), half), :] = other_ref[...]


def norm_kernel(x_ref, normed_t_ref, normed_ref, gram_ref):
    xfloat = x_ref[...].astype(f32)
    mean = jnp.mean(xfloat * xfloat, axis=0, keepdims=True)
    scaled = (xfloat * lax.rsqrt(mean + 1e-06)).astype(bf16)
    normed_t_ref[...] = scaled
    flat = scaled.T
    normed_ref[...] = flat
    gram_ref[...] = mm_nt(flat, flat)


def block(j):
    return pl.ds(j * PART, PART)


def first_kernel(
    wait, core_ref, normed, own_ref, goal_ref, up_ref, down_ref,
    pre_ref, act_ref, keep_ref, send_ref,
    total, wide,
):
    total[...] = place_gap(core_ref, own_ref, goal_ref, 0, wide)
    for j in range(BLOCKS):
        wait(0, j)
        pre = mm(normed[...], up_ref[:, block(j)])
        pre_ref[:, block(j)] = pre
        act_ref[:, block(j)] = gelu_parts(pre[:TOK])[0].astype(bf16)
    for j in range(BLOCKS):
        wait(1, j)
    for j in range(BLOCKS):
        total[:, block(j)] += mm(act_ref[...], down_ref[:, block(j)])
    hand_out(core_ref, total, keep_ref, send_ref)


def second_kernel(
    wait, core_ref, mine_ref, other_ref, own_ref, goal_ref, down_ref, pre_ref, act_ref, gram_ref,
    resid_ref, resid_t_ref, dpre_ref, pre_2_ref, act_2_ref, keep_ref, send_ref,
    total, wide,
):
    take_in(core_ref, mine_ref, other_ref, resid_ref)
    for j in range(BLOCKS):
        wait(0, j)
        back = mm_nt(resid_ref[...], down_ref[block(j), :])
        dpre_ref[:, block(j)] = (back * gelu_parts(pre_ref[:TOK, block(j)])[1]).astype(bf16)
    for j in range(BLOCKS):
        pre_2 = pre_ref[TOK:, block(j)] - local_rate * mm_split(
            gram_ref[TOK:, :TOK], dpre_ref[:, block(j)]
        )
        pre_2_ref[:, block(j)] = pre_2
        act_2_ref[:, block(j)] = gelu_parts(pre_2)[0].astype(bf16)
    total[...] = place_gap(core_ref, own_ref, goal_ref, 1, wide)
    cross = mm_nt(act_2_ref[...], act_ref[...])
    for j in range(BLOCKS):
        total[:, block(j)] += mm(act_2_ref[...], down_ref[:, block(j)]) - local_rate * mm_split(
            cross, resid_ref[:, block(j)]
        )
    hand_out(core_ref, total, keep_ref, send_ref)
    resid_t_ref[...] = resid_ref[...].T


def third_kernel(
    wait, core_ref, mine_ref, other_ref, resid_ref, down_ref, act_ref, act_2_ref, pre_2_ref, dpre_ref, gram_ref,
    resid_t_ref, dpre_2_ref, squared_ref,
    resid_2,
):
    take_in(core_ref, mine_ref, other_ref, resid_2)
    both = jnp.concatenate([resid_ref[...], resid_2[...]], axis=0)
    gram_resid = mm_nt(both, both)
    for j in range(BLOCKS):
        wait(0, j)
        back = mm_nt(resid_2[...], down_ref[block(j), :]) - local_rate * mm_split(
            gram_resid[TOK:, :TOK], act_ref[:, block(j)]
        )
        dpre_2_ref[:, block(j)] = (back * gelu_parts(pre_2_ref[:, block(j)])[1]).astype(bf16)
    acts = jnp.concatenate([act_ref[...], act_2_ref[...]], axis=0)
    dpres = jnp.concatenate([dpre_ref[...], dpre_2_ref[...]], axis=0)
    terms = gram_ref[...] * mm_nt(dpres, dpres) + gram_resid * mm_nt(acts, acts)
    squared_ref[...] = jnp.full((8, 128), (local_rate * local_rate) * jnp.sum(terms), f32)
    resid_t_ref[...] = resid_2[...].T


def whole(ref, j):
    return ref


def columns(ref, j):
    return ref.at[:, pl.ds(j * PART, PART)]


def rows(ref, j):
    return ref.at[pl.ds(j * PART, PART), :]


def weight_columns(ref, j):
    return columns(ref, j)


def weight_rows(ref, j):
    return rows(ref, j)


HALF_TOK = (TOK // 2, D)


def call(kernel, views, out_types, scratch, flops, moved):
    weights = [i for i, view in enumerate(views) if view in (weight_rows, weight_columns)]
    def body(*refs):
        refs = list(refs)
        own = refs[len(views) : len(views) + len(scratch)]
        held = refs[len(views) + len(scratch) :]
        copies = {}
        for n, i in enumerate(weights):
            for j in range(BLOCKS):
                copies[n, j] = pltpu.make_async_copy(
                    views[i](refs[i], j), views[i](held[2 * n], j), held[2 * n + 1].at[j]
                )
                copies[n, j].start()
            refs[i] = held[2 * n]
        kernel(lambda n, j: copies[n, j].wait(), *refs[: len(views)], *own)

    vmem = pl.BlockSpec(memory_space=pltpu.VMEM)
    smem = pl.BlockSpec(memory_space=pltpu.SMEM)
    return pl.pallas_call(
        body,
        in_specs=[smem]
        + [
            pl.BlockSpec(memory_space=pl.ANY) if i in weights else vmem
            for i in range(1, len(views) - len(out_types))
        ],
        out_specs=[vmem] * len(out_types),
        out_shape=[jax.ShapeDtypeStruct(*kind) for kind in out_types],
        scratch_shapes=[pltpu.VMEM(*kind) for kind in scratch]
        + [pltpu.VMEM((D, D), bf16), pltpu.SemaphoreType.DMA((BLOCKS,))] * len(weights),
        compiler_params=pltpu.CompilerParams(vmem_limit_bytes=VMEM_BYTES),
        cost_estimate=pl.CostEstimate(flops=flops, bytes_accessed=moved, transcendentals=0),
    )


def reduce_over_tp(keep, send):
    got = lax.ppermute(send, "tp", CORE_SWAP).astype(f32)
    chip = (keep + got).astype(bf16)
    far = lax.ppermute(chip, "tp", FAR_SWAP)
    mine = ((chip.astype(f32) + far.astype(f32)) * (1.0 / TOK)).astype(bf16)
    return mine, lax.ppermute(mine, "tp", CORE_SWAP)


def ring(piece, axis, up, down, me, n, farthest=None):
    far = n // 2
    opposite = (farthest or piece)((me + far) % n).astype(bf16)
    got = (
        lax.ppermute(opposite[..., :HALF], axis, up),
        lax.ppermute(opposite[..., HALF:], axis, down),
    )
    for distance in range(far - 1, 0, -1):
        got = yield got
        from_down, from_up = [array.astype(f32) for array in got]
        ahead = piece((me + distance) % n)
        behind = piece((me + n - distance) % n)
        if distance == far - 1:
            ahead = jnp.concatenate(
                [ahead[..., :HALF] + from_down, ahead[..., HALF:]], axis=-1
            )
            behind = jnp.concatenate(
                [behind[..., :HALF], behind[..., HALF:] + from_up], axis=-1
            )
        else:
            ahead = ahead + from_down
            behind = behind + from_up
        ahead, behind = yield (ahead.astype(bf16), behind.astype(bf16))
        got = (lax.ppermute(ahead, axis, up), lax.ppermute(behind, axis, down))
    got = yield got
    return piece(me) + got[0].astype(f32) + got[1].astype(f32)


def finish(steps, pair):
    try:
        while True:
            pair = steps.send(pair)
    except StopIteration as end:
        return end.value


def swap_y(block, y_lo):
    halves = block.reshape(2, BLOCK // 2, D)
    mine = jnp.where(y_lo == 0, halves[0], halves[1])
    other = jnp.where(y_lo == 0, halves[1], halves[0]).astype(bf16)
    return mine + lax.ppermute(other, "region", Y_SWAP).astype(f32)


def shards(hidden_in, target, up_weight, down_weight, noise_up, noise_down):
    tp = lax.axis_index("tp")
    client = lax.axis_index("client")
    region = lax.axis_index("region")
    z = region // 2
    y_lo = region % 2

    own = jnp.swapaxes(hidden_in[0], 1, 2)
    goal = jnp.swapaxes(target[0], 1, 2)
    states = lax.all_gather(
        jnp.concatenate([own[0], own[1]], axis=1), "tp", axis=0, tiled=True
    )
    spot = tp.astype(jnp.int32).reshape(1)

    normed_t, normed, gram = pl.pallas_call(
        norm_kernel,
        out_shape=[
            jax.ShapeDtypeStruct((D, 2 * TOK), bf16),
            jax.ShapeDtypeStruct((2 * TOK, D), bf16),
            jax.ShapeDtypeStruct((2 * TOK, 2 * TOK), f32),
        ],
        compiler_params=pltpu.CompilerParams(vmem_limit_bytes=VMEM_BYTES),
    )(states)
    pre, act_1, keep, send = call(
        first_kernel,
        [whole, whole, whole, whole, weight_columns, weight_rows] + [columns, columns, whole, whole],
        [((2 * TOK, D), f32), ((TOK, D), bf16), (HALF_TOK, f32), (HALF_TOK, bf16)],
        [((TOK, D), f32), ((D, TOK), f32)],
        6 * TOK * D * D, 4 * D * D,
    )(spot, normed, own, goal, up_weight, down_weight)
    mine, other = reduce_over_tp(keep, send)

    resid_1, resid_t_1, dpre_1, pre_2, act_2, keep, send = call(
        second_kernel,
        [whole, whole, whole, whole, whole, weight_rows, columns, columns, whole]
        + [whole, whole, columns, columns, columns, whole, whole],
        [((TOK, D), bf16), ((D, TOK), bf16), ((TOK, D), bf16), ((TOK, D), f32), ((TOK, D), bf16), (HALF_TOK, f32), (HALF_TOK, bf16)],
        [((TOK, D), f32), ((D, TOK), f32)],
        4 * TOK * D * D, 2 * D * D,
    )(spot, mine, other, own, goal, down_weight, pre, act_1, gram)
    mine, other = reduce_over_tp(keep, send)

    resid_t_2, dpre_2, squared = call(
        third_kernel,
        [whole, whole, whole, whole, weight_rows, columns, columns, columns, columns, whole]
        + [whole, columns, whole],
        [((D, TOK), bf16), ((TOK, D), bf16), ((8, 128), f32)],
        [((TOK, D), bf16)],
        2 * TOK * D * D, 2 * D * D,
    )(spot, mine, other, resid_1, down_weight, act_1, act_2, pre_2, dpre_1, gram)
    acts = jnp.concatenate([act_1, act_2], axis=0)
    dpres = jnp.concatenate([dpre_1, dpre_2], axis=0)
    resids_t = jnp.concatenate([resid_t_1, resid_t_2], axis=1)

    rows_up = normed_t.reshape(4, 8, BLOCK, 2 * TOK)
    rows_down = resids_t.reshape(4, 8, BLOCK, 2 * TOK)

    def up_raw(k):
        picked = lax.dynamic_index_in_dim(rows_up, k, 0, keepdims=False)
        return -local_rate * mm(picked.reshape(8 * BLOCK, 2 * TOK), dpres)

    def up_piece(k):
        return factor * up_raw(k)

    def down_piece(k):
        picked = lax.dynamic_index_in_dim(rows_down, k, 1, keepdims=False)
        return (-local_rate * factor) * mm(picked.reshape(4 * BLOCK, 2 * TOK), acts)

    along_x = ring(up_piece, "client", X_UP, X_DOWN, client, 4, up_raw)
    arriving = next(along_x)

    squared = squared + lax.ppermute(squared, "tp", CORE_SWAP)
    squared = squared + lax.ppermute(squared, "tp", FAR_SWAP)
    bound = clip_rms * math.sqrt(2.0 * D * F)
    factors = bound / jnp.maximum(jnp.sqrt(squared), bound)
    factor = factors[0, 0]
    along_z = ring(down_piece, "region", Z_UP, Z_DOWN, z, 8)
    arriving_z = next(along_z)
    factor_below = lax.ppermute(factors, "client", X_UP)[0, 0]
    factor_above = lax.ppermute(factors, "client", X_DOWN)[0, 0]
    leaving = along_z.send(arriving_z)
    arrived = (arriving[0].astype(f32) * factor_below, arriving[1].astype(f32) * factor_above)
    down_z = finish(along_z, leaving)
    up_x = finish(along_x, along_x.send(arrived))
    up_x = up_x.reshape(8, BLOCK, D)
    down_z = down_z.reshape(4, BLOCK, D)

    def at(array):
        return lambda k: lax.dynamic_index_in_dim(array, k, 0, keepdims=False)

    along_z = ring(at(up_x), "region", Z_UP, Z_DOWN, z, 8)
    along_x = ring(at(down_z), "client", X_UP, X_DOWN, client, 4)
    up_z = finish(along_z, next(along_z))
    down_x = finish(along_x, next(along_x))
    total_up = swap_y(up_z, y_lo)
    total_down = swap_y(down_x, y_lo).T

    count = 64
    width = D // count
    block = client * 16 + region
    base_up = lax.dynamic_slice_in_dim(up_weight, block * width, width, 0).astype(f32)
    base_down = lax.dynamic_slice_in_dim(down_weight, block * width, width, 1).astype(f32)
    root = math.sqrt(count)
    scale = server_rate / (clip_rms * root)
    new_up = base_up + scale * (total_up + clip_rms * root * noise_up)
    new_down = base_down + scale * (total_down + clip_rms * root * noise_down)
    return (new_up, new_down)


def solution(mesh):
    placed = (
        P(("client", "region"), None, None, "tp"),
        P(("client", "region"), None, None, "tp"),
        P(None, "tp"),
        P("tp", None),
        P(("client", "region"), "tp"),
        P("tp", ("client", "region")),
    )
    return jax.shard_map(
        shards,
        mesh=mesh,
        in_specs=placed,
        out_specs=(P(("client", "region"), "tp"), P("tp", ("client", "region"))),
        check_vma=False,
    )
```

```python
import math

import jax
import jax.numpy as jnp
from jax import lax
from jax.experimental import pallas as pl
from jax.experimental.pallas import tpu as pltpu
from jax.sharding import PartitionSpec as P

D = 1792
F = 7168
TOK = 128
HALF = 896
BLOCK = 56
PART = 256
BLOCKS = D // PART
VMEM_BYTES = 48 * 1024 * 1024
ROOT_2_PI = math.sqrt(2.0 / math.pi)

local_rate = 0.5
clip_rms = 0.08
server_rate = 0.02

X_UP = [(i, (i + 1) % 4) for i in range(4)]
X_DOWN = [(i, (i + 3) % 4) for i in range(4)]
Z_UP = [(i, (i + 2) % 16) for i in range(16)]
Z_DOWN = [(i, (i + 14) % 16) for i in range(16)]
Y_SWAP = [(i, i ^ 1) for i in range(16)]
CORE_SWAP = [(i, i ^ 1) for i in range(4)]
FAR_SWAP = [(i, i ^ 2) for i in range(4)]

f32 = jnp.float32
bf16 = jnp.bfloat16


def mm(left, right):
    return jnp.dot(left, right, preferred_element_type=f32)


def mm_nt(left, right):
    return lax.dot_general(left, right, (((1,), (1,)), ((), ())), preferred_element_type=f32)


def mm_split(left, right):
    high = left.astype(bf16)
    low = (left - high.astype(f32)).astype(bf16)
    return mm(high, right) + mm(low, right)


def gelu_parts(pre):
    square = pre * pre
    curve = jnp.tanh(ROOT_2_PI * (pre + 0.044715 * pre * square))
    value = 0.5 * pre * (1.0 + curve)
    slope = 0.5 * (1.0 + curve) + 0.5 * pre * (1.0 - curve * curve) * (
        ROOT_2_PI * (1.0 + 3.0 * 0.044715 * square)
    )
    return value, slope


def place_gap(core_ref, own_ref, goal_ref, step, wide):
    wide[...] = jnp.zeros_like(wide)
    start = pl.multiple_of(core_ref[0] * (D // 4), 64)
    wide[pl.ds(start, D // 4), :] = own_ref[step].astype(f32) - goal_ref[step].astype(f32)
    return wide[...].T


def hand_out(core_ref, total, keep_ref, send_ref):
    core = core_ref[0] % 2
    half = TOK // 2
    keep_ref[...] = total[pl.ds(pl.multiple_of(core * half, half), half), :]
    other = total[pl.ds(pl.multiple_of((1 - core) * half, half), half), :]
    send_ref[...] = other.astype(bf16)


def take_in(core_ref, mine_ref, other_ref, resid):
    core = core_ref[0] % 2
    half = TOK // 2
    resid[pl.ds(pl.multiple_of(core * half, half), half), :] = mine_ref[...]
    resid[pl.ds(pl.multiple_of((1 - core) * half, half), half), :] = other_ref[...]


def norm_kernel(x_ref, normed_t_ref, normed_ref, gram_ref):
    xfloat = x_ref[...].astype(f32)
    mean = jnp.mean(xfloat * xfloat, axis=0, keepdims=True)
    scaled = (xfloat * lax.rsqrt(mean + 1e-06)).astype(bf16)
    normed_t_ref[...] = scaled
    flat = scaled.T
    normed_ref[...] = flat
    gram_ref[...] = mm_nt(flat, flat)


def first_kernel(
    j, core_ref, normed, own_ref, goal_ref, up_ref, down_ref,
    pre_ref, act_ref, keep_ref, send_ref,
    total, wide,
):
    @pl.when(j == 0)
    def _():
        total[...] = place_gap(core_ref, own_ref, goal_ref, 0, wide)

    pre = mm(normed[...], up_ref[...])
    pre_ref[...] = pre
    act = gelu_parts(pre[:TOK])[0].astype(bf16)
    act_ref[...] = act
    total[...] += mm(act, down_ref[...])

    @pl.when(j == BLOCKS - 1)
    def _():
        hand_out(core_ref, total, keep_ref, send_ref)


def second_kernel(
    j, core_ref, mine_ref, other_ref, own_ref, goal_ref, down_ref, pre_ref, act_ref, gram_ref,
    resid_ref, resid_t_ref, dpre_ref, pre_2_ref, act_2_ref, keep_ref, send_ref,
    total, wide, cross,
):

    @pl.when(j == 0)
    def _():
        take_in(core_ref, mine_ref, other_ref, resid_ref)
        total[...] = place_gap(core_ref, own_ref, goal_ref, 1, wide)
        cross[...] = jnp.zeros_like(cross)
        resid_t_ref[...] = resid_ref[...].T

    back = mm_nt(resid_ref[...], down_ref[...])
    dpre = (back * gelu_parts(pre_ref[:TOK, :])[1]).astype(bf16)
    dpre_ref[...] = dpre
    pre_2 = pre_ref[TOK:, :] - local_rate * mm_split(gram_ref[TOK:, :TOK], dpre)
    pre_2_ref[...] = pre_2
    act_2 = gelu_parts(pre_2)[0].astype(bf16)
    act_2_ref[...] = act_2
    total[...] += mm(act_2, down_ref[...])
    cross[...] += mm_nt(act_2, act_ref[...])

    @pl.when(j == BLOCKS - 1)
    def _():
        total[...] -= local_rate * mm_split(cross[...], resid_ref[...])
        hand_out(core_ref, total, keep_ref, send_ref)


def third_kernel(
    j, core_ref, mine_ref, other_ref, resid_ref, down_ref, act_ref, act_2_ref, pre_2_ref, dpre_ref, gram_ref,
    resid_t_ref, dpre_2_ref, squared_ref,
    resid_2, gram_resid, gram_act, gram_dpre,
):

    @pl.when(j == 0)
    def _():
        take_in(core_ref, mine_ref, other_ref, resid_2)
        both = jnp.concatenate([resid_ref[...], resid_2[...]], axis=0)
        gram_resid[...] = mm_nt(both, both)
        gram_act[...] = jnp.zeros_like(gram_act)
        gram_dpre[...] = jnp.zeros_like(gram_dpre)
        resid_t_ref[...] = resid_2[...].T

    back = mm_nt(resid_2[...], down_ref[...]) - local_rate * mm_split(
        gram_resid[TOK:, :TOK], act_ref[...]
    )
    dpre_2 = (back * gelu_parts(pre_2_ref[...])[1]).astype(bf16)
    dpre_2_ref[...] = dpre_2
    acts = jnp.concatenate([act_ref[...], act_2_ref[...]], axis=0)
    gram_act[...] += mm_nt(acts, acts)
    dpres = jnp.concatenate([dpre_ref[...], dpre_2], axis=0)
    gram_dpre[...] += mm_nt(dpres, dpres)

    @pl.when(j == BLOCKS - 1)
    def _():
        terms = gram_ref[...] * gram_dpre[...] + gram_resid[...] * gram_act[...]
        squared_ref[...] = jnp.full((8, 128), (local_rate * local_rate) * jnp.sum(terms), f32)


def whole(ref, j):
    return ref


def columns(ref, j):
    return ref.at[:, pl.ds(j * PART, PART)]


def rows(ref, j):
    return ref.at[pl.ds(j * PART, PART), :]


HALF_TOK = (TOK // 2, D)


def call(kernel, views, out_types, scratch, flops, moved):
    def body(*refs):
        for j in range(BLOCKS):
            seen = [view(ref, j) for view, ref in zip(views, refs)]
            kernel(j, *seen, *refs[len(views) :])

    vmem = pl.BlockSpec(memory_space=pltpu.VMEM)
    smem = pl.BlockSpec(memory_space=pltpu.SMEM)
    return pl.pallas_call(
        body,
        in_specs=[smem] + [vmem] * (len(views) - len(out_types) - 1),
        out_specs=[vmem] * len(out_types),
        out_shape=[jax.ShapeDtypeStruct(*kind) for kind in out_types],
        scratch_shapes=[pltpu.VMEM(*kind) for kind in scratch],
        compiler_params=pltpu.CompilerParams(vmem_limit_bytes=VMEM_BYTES),
        cost_estimate=pl.CostEstimate(flops=flops, bytes_accessed=moved, transcendentals=0),
    )


def reduce_over_tp(keep, send):
    got = lax.ppermute(send, "tp", CORE_SWAP).astype(f32)
    chip = (keep + got).astype(bf16)
    far = lax.ppermute(chip, "tp", FAR_SWAP)
    mine = ((chip.astype(f32) + far.astype(f32)) * (1.0 / TOK)).astype(bf16)
    return mine, lax.ppermute(mine, "tp", CORE_SWAP)


def ring(piece, axis, up, down, me, n):
    far = n // 2
    opposite = piece((me + far) % n)
    from_down = lax.ppermute(opposite[..., :HALF].astype(bf16), axis, up)
    from_up = lax.ppermute(opposite[..., HALF:].astype(bf16), axis, down)
    for distance in range(far - 1, 0, -1):
        ahead = piece((me + distance) % n)
        behind = piece((me + n - distance) % n)
        if distance == far - 1:
            ahead = jnp.concatenate(
                [ahead[..., :HALF] + from_down.astype(f32), ahead[..., HALF:]], axis=-1
            )
            behind = jnp.concatenate(
                [behind[..., :HALF], behind[..., HALF:] + from_up.astype(f32)], axis=-1
            )
        else:
            ahead = ahead + from_down.astype(f32)
            behind = behind + from_up.astype(f32)
        from_down = lax.ppermute(ahead.astype(bf16), axis, up)
        from_up = lax.ppermute(behind.astype(bf16), axis, down)
    return piece(me) + from_down.astype(f32) + from_up.astype(f32)


def swap_y(block, y_lo):
    halves = block.reshape(2, BLOCK // 2, D)
    mine = jnp.where(y_lo == 0, halves[0], halves[1])
    other = jnp.where(y_lo == 0, halves[1], halves[0]).astype(bf16)
    return mine + lax.ppermute(other, "region", Y_SWAP).astype(f32)


def shards(hidden_in, target, up_weight, down_weight, noise_up, noise_down):
    tp = lax.axis_index("tp")
    client = lax.axis_index("client")
    region = lax.axis_index("region")
    z = region // 2
    y_lo = region % 2

    own = jnp.swapaxes(hidden_in[0], 1, 2)
    goal = jnp.swapaxes(target[0], 1, 2)
    states = lax.all_gather(
        jnp.concatenate([own[0], own[1]], axis=1), "tp", axis=0, tiled=True
    )
    spot = tp.astype(jnp.int32).reshape(1)

    normed_t, normed, gram = pl.pallas_call(
        norm_kernel,
        out_shape=[
            jax.ShapeDtypeStruct((D, 2 * TOK), bf16),
            jax.ShapeDtypeStruct((2 * TOK, D), bf16),
            jax.ShapeDtypeStruct((2 * TOK, 2 * TOK), f32),
        ],
        compiler_params=pltpu.CompilerParams(vmem_limit_bytes=VMEM_BYTES),
    )(states)
    pre, act_1, keep, send = call(
        first_kernel,
        [whole, whole, whole, whole, columns, rows] + [columns, columns, whole, whole],
        [((2 * TOK, D), f32), ((TOK, D), bf16), (HALF_TOK, f32), (HALF_TOK, bf16)],
        [((TOK, D), f32), ((D, TOK), f32)],
        6 * TOK * D * D, 4 * D * D,
    )(spot, normed, own, goal, up_weight, down_weight)
    mine, other = reduce_over_tp(keep, send)

    resid_1, resid_t_1, dpre_1, pre_2, act_2, keep, send = call(
        second_kernel,
        [whole, whole, whole, whole, whole, rows, columns, columns, whole]
        + [whole, whole, columns, columns, columns, whole, whole],
        [((TOK, D), bf16), ((D, TOK), bf16), ((TOK, D), bf16), ((TOK, D), f32), ((TOK, D), bf16), (HALF_TOK, f32), (HALF_TOK, bf16)],
        [((TOK, D), f32), ((D, TOK), f32), ((TOK, TOK), f32)],
        4 * TOK * D * D, 2 * D * D,
    )(spot, mine, other, own, goal, down_weight, pre, act_1, gram)
    mine, other = reduce_over_tp(keep, send)

    resid_t_2, dpre_2, squared = call(
        third_kernel,
        [whole, whole, whole, whole, rows, columns, columns, columns, columns, whole]
        + [whole, columns, whole],
        [((D, TOK), bf16), ((TOK, D), bf16), ((8, 128), f32)],
        [((TOK, D), bf16)] + [((2 * TOK, 2 * TOK), f32)] * 3,
        2 * TOK * D * D, 2 * D * D,
    )(spot, mine, other, resid_1, down_weight, act_1, act_2, pre_2, dpre_1, gram)
    acts = jnp.concatenate([act_1, act_2], axis=0)
    dpres = jnp.concatenate([dpre_1, dpre_2], axis=0)
    resids_t = jnp.concatenate([resid_t_1, resid_t_2], axis=1)

    squared = squared + lax.ppermute(squared, "tp", CORE_SWAP)
    squared = squared + lax.ppermute(squared, "tp", FAR_SWAP)
    squared = squared[0, 0]
    bound = clip_rms * math.sqrt(2.0 * D * F)
    factor = bound / jnp.maximum(jnp.sqrt(squared), bound)
    scale_own = -local_rate * factor

    rows_up = normed_t.reshape(4, 8, BLOCK, 2 * TOK)
    rows_down = resids_t.reshape(4, 8, BLOCK, 2 * TOK)

    def up_piece(k):
        rows = lax.dynamic_index_in_dim(rows_up, k, 0, keepdims=False)
        return scale_own * mm(rows.reshape(8 * BLOCK, 2 * TOK), dpres)

    def down_piece(k):
        rows = lax.dynamic_index_in_dim(rows_down, k, 1, keepdims=False)
        return scale_own * mm(rows.reshape(4 * BLOCK, 2 * TOK), acts)

    up_x = ring(up_piece, "client", X_UP, X_DOWN, client, 4)
    down_z = ring(down_piece, "region", Z_UP, Z_DOWN, z, 8)
    up_x = up_x.reshape(8, BLOCK, D)
    down_z = down_z.reshape(4, BLOCK, D)

    def at(array):
        return lambda k: lax.dynamic_index_in_dim(array, k, 0, keepdims=False)

    up_z = ring(at(up_x), "region", Z_UP, Z_DOWN, z, 8)
    down_x = ring(at(down_z), "client", X_UP, X_DOWN, client, 4)
    total_up = swap_y(up_z, y_lo)
    total_down = swap_y(down_x, y_lo).T

    count = 64
    width = D // count
    block = client * 16 + region
    base_up = lax.dynamic_slice_in_dim(up_weight, block * width, width, 0).astype(f32)
    base_down = lax.dynamic_slice_in_dim(down_weight, block * width, width, 1).astype(f32)
    root = math.sqrt(count)
    scale = server_rate / (clip_rms * root)
    new_up = base_up + scale * (total_up + clip_rms * root * noise_up)
    new_down = base_down + scale * (total_down + clip_rms * root * noise_down)
    return (new_up, new_down)


def solution(mesh):
    placed = (
        P(("client", "region"), None, None, "tp"),
        P(("client", "region"), None, None, "tp"),
        P(None, "tp"),
        P("tp", None),
        P(("client", "region"), "tp"),
        P("tp", ("client", "region")),
    )
    return jax.shard_map(
        shards,
        mesh=mesh,
        in_specs=placed,
        out_specs=(P(("client", "region"), "tp"), P("tp", ("client", "region"))),
        check_vma=False,
    )
```
